256 devices in a mesh: grid: 32 (over y_hi, z, core), chan: 8 (over x, y_lo).
Axes of the slice: x: 4, y: 4 (y_hi: 2, y_lo: 2; y = y_hi * 2 + y_lo), z: 8, core: 2. Of those that a mesh axis runs over, the one named last changes fastest.
Arguments:
- activations: bfloat16 [256, 32, 8, 16, 128], P('chan', 'grid'), may hold values from -6 to 6
- grad_out: bfloat16 [256, 32, 16, 128], P('chan', 'grid'), may hold values from -6 to 6
- weight: bfloat16 [27, 256, 256], P(None, 'chan'), may hold values from -0.078125 to 0.078125
Outputs:
- grad_act: bfloat16 [256, 32, 8, 16, 128], P('chan', 'grid')
- grad_weight: float32 [27, 256, 256], P(None, 'chan')
The draws below stay inside these ranges and needn't reach their ends.
All inputs are finite; a program needn't handle non-finite values.
Results may differ from the reference program's by a relative error of at most 0.001.
Values may be sent and summed in bfloat16 or wider, within the bound.
A program may use at most 64 MiB of HBM per device.

```python
import math
import jax
import jax.numpy as jnp

CIN = 256
COUT = 256
YO = 16
ZO = 128
XO = 32


def steps_of(rng, shape, cuts, low, largest):
    loudness, own = 1.0, jax.random.fold_in(rng, 6)
    for position, parts in cuts:
        steps = jnp.exp(jax.random.uniform(jax.random.fold_in(own, position), (parts,), jnp.float32, low / len(cuts), largest / len(cuts)))
        loudness = loudness * jnp.repeat(steps, shape[position] // parts).reshape([-1 if axis == position else 1 for axis in range(len(shape))])
    return loudness


def gaussian(rng, extent, scale, most, split=(), held_as=jnp.bfloat16):
    loudness = steps_of(rng, extent, split, -0.22, 0.18) if split else 1.0
    values = jax.random.normal(rng, extent, jnp.float32) * scale * loudness
    return jnp.minimum(jnp.maximum(values, -most), most).astype(held_as)


def setup_inputs(seed: int = 0) -> dict:
    key_of = jax.random.split(jax.random.key(seed), 4)
    return {
        "activations": gaussian(key_of[0], (CIN, XO, 8, YO, ZO), 1.0, 6.0, ((0, 8), (1, 32))),
        "grad_out": gaussian(key_of[1], (COUT, XO, YO, ZO), 1.0, 6.0, ((0, 8), (1, 32))),
        "weight": gaussian(key_of[2], (27, CIN, COUT), (27 * CIN) ** -0.5, 0.078125, ((1, 8),)),
    }


def parity_taps(parity):
    if parity == 0:
        return [(1, 0)]
    return [(2, 0), (0, 1)]

def tap_parity(tap):
    if tap == 1:
        return (0, 0)
    if tap == 2:
        return (1, 0)
    return (1, 1)

def shifted_grads(grad_cells, rim_plane):
    result = {}
    for step_x in range(2):
        if step_x == 0:
            x_shifted = grad_cells
        else:
            x_shifted = jnp.concatenate([grad_cells[:, 1:], rim_plane[:, None]], 1)
        for step_y in range(2):
            if step_y == 0:
                y_shifted = x_shifted
            else:
                y_shifted = jnp.concatenate([x_shifted[:, :, 1:], jnp.zeros_like(x_shifted[:, :, :1])], 2)
            for step_z in range(2):
                if step_z == 0:
                    z_shifted = y_shifted
                else:
                    z_shifted = jnp.concatenate([y_shifted[:, :, :, 1:], jnp.zeros_like(y_shifted[:, :, :, :1])], 3)
                result[step_x, step_y, step_z] = z_shifted
    return result

def reference(activations, grad_out, weight):
    channels = activations.shape[0]
    count_out = XO * YO * ZO
    rim_plane = jnp.zeros_like(grad_out[:, 0])
    shifted = shifted_grads(grad_out, rim_plane)
    terms = []
    for tap_index in range(27):
        par_x, step_x = tap_parity(tap_index // 9)
        par_y, step_y = tap_parity(tap_index // 3 % 3)
        par_z, step_z = tap_parity(tap_index % 3)
        act_slab = activations[:, :, 4 * par_x + 2 * par_y + par_z].astype(jnp.float32)
        grad_slab = shifted[step_x, step_y, step_z].astype(jnp.float32)
        terms.append(jnp.einsum('cxyz,oxyz->co', act_slab, grad_slab))
    grad_weight = jnp.stack(terms, 0) * (1.0 / math.sqrt(count_out))
    blocks = []
    for parity in range(8):
        par_x, par_y, par_z = (parity // 4, parity // 2 % 2, parity % 2)
        block_sum = jnp.zeros((channels, count_out), jnp.float32)
        for tap_x, step_x in parity_taps(par_x):
            for tap_y, step_y in parity_taps(par_y):
                for tap_z, step_z in parity_taps(par_z):
                    window = shifted[step_x, step_y, step_z].reshape(COUT, count_out)
                    block_sum = block_sum + jnp.dot(weight[tap_x * 9 + tap_y * 3 + tap_z], window, preferred_element_type=jnp.float32)
        blocks.append(block_sum.reshape(channels, XO, YO, ZO))
    grad_act = jnp.stack(blocks, 2).astype(jnp.bfloat16)
    return (grad_act, grad_weight)
```

```python
import math

import jax
import jax.numpy as jnp
from jax import lax
from jax.experimental import pallas as pl
from jax.experimental.pallas import tpu as pltpu
from jax.sharding import PartitionSpec as P

MESH = pl.DeviceIdType.MESH
F32, BF16 = jnp.float32, jnp.bfloat16
NX, NYL, NZ, NYH = 4, 2, 8, 2
Y, Z = 16, 128
CELLS = Y * Z
PAD = 32
SPAN = 240.0


def tap_of(par, step):
    if par == 0:
        return 1 if step == 0 else None
    return 2 if step == 0 else 0


def taps_of_shift(shift):
    found = []
    for par in range(8):
        bits = (par // 4, par // 2 % 2, par % 2)
        taps = [tap_of(b, s) for b, s in zip(bits, shift)]
        if None not in taps:
            found.append((par, 9 * taps[0] + 3 * taps[1] + taps[2]))
    return found


SHIFTS = [(sx, sy, sz) for sx in range(2) for sy in range(2) for sz in range(2)]


def encode(values):
    largest = jnp.max(jnp.abs(values), axis=1, keepdims=True)
    scale = jnp.maximum((largest * 1.01).astype(BF16).astype(F32), 1e-30)
    level = values * (SPAN / scale)
    power = jnp.exp2(jnp.abs(level) - SPAN / 2)
    power = jnp.where(values < 0, -power, power)
    row = lax.broadcasted_iota(jnp.int32, values.shape, 1)
    return jnp.where(row >= 27, scale, power).astype(BF16)


def decode(codes):
    codes = codes.astype(F32)
    scale = codes[:, 27:28] * (1.0 / SPAN)
    level = (jnp.log2(jnp.abs(codes)) + SPAN / 2) * scale
    return jnp.where(codes < 0, -level, level)


def kernel(
    norm, act_ref, grad_ref, weight_ref, out_act, out_w,
    rows32, acts, grads, dense, terms, from_mate, rs_own, rs_out, rs_in, ag, final,
    send_own, recv_own, send_rim, recv_rim, mate_send, mate_recv,
    rs_send, rs_recv, ag_send, ag_recv, fw_send, fw_recv,
):
    g, chan = lax.axis_index("grid"), lax.axis_index("chan")
    yh, z, core = g // (2 * NZ), (g // 2) % NZ, g % 2
    x, yl = chan // NYL, chan % NYL
    w = yh * NZ + z

    def chan_of(dx, dy):
        return lax.rem(x + dx, NX) * NYL + lax.rem(yl + dy, NYL)

    def at_chan(dx, dy):
        return (g, chan_of(dx, dy))

    mate = (g + 1 - 2 * core, chan)
    before = (jnp.maximum(g - 1, 0), chan)

    def peer_w(d):
        a, k = d // NZ, d % NZ
        return lax.rem(yh + a, NYH) * NZ + lax.rem(z + k, NZ)

    def peer(d):
        return (peer_w(d) * 2 + core, chan)

    has_rim = jnp.logical_and(core == 1, g < 2 * NZ * NYH - 1)
    gives_rim = jnp.logical_and(core == 0, g > 0)

    barrier = pltpu.get_barrier_semaphore()
    near = [at_chan(1, 0), at_chan(3, 0), at_chan(2, 0), at_chan(0, 1), mate]
    near += [peer(d) for d in range(1, NZ * NYH)]
    for device in near:
        pl.semaphore_signal(barrier, inc=1, device_id=device, device_id_type=MESH)

    @pl.when(gives_rim)
    def _():
        pl.semaphore_signal(barrier, inc=1, device_id=before, device_id_type=MESH)

    @pl.when(has_rim)
    def _():
        pl.semaphore_signal(barrier, inc=1, device_id=(g + 1, chan), device_id_type=MESH)

    def shard(plane, dx, dy):
        start = pl.multiple_of(chan_of(dx, dy) * 32, 32)
        return grads.at[plane, 0, pl.ds(start, 32), pl.ds(0, CELLS)]

    rows32[0 : 32 * Y] = grad_ref[:, 0].astype(F32).reshape(32 * Y, Z)
    start_own = pl.multiple_of(chan * 32, 32)
    for j in range(Y):
        grads[0, 0, pl.ds(start_own, 32), j * Z : (j + 1) * Z] = rows32[
            pl.ds(j, 32, stride=Y)
        ].astype(BF16)

    rim_partners = jnp.logical_or(gives_rim, has_rim).astype(jnp.int32)
    pl.semaphore_wait(barrier, len(near) + rim_partners)

    def copy(src, dst, send, recv, device):
        return pltpu.make_async_remote_copy(
            src_ref=src, dst_ref=dst, send_sem=send, recv_sem=recv,
            device_id=device, device_id_type=MESH,
        )

    def gather_copies(plane, send, recv):
        def one(n, dx, dy, slot, device):
            return copy(
                shard(plane, dx, dy), shard(plane, dx, dy), send.at[n], recv.at[slot], device
            )

        own = [
            one(0, 0, 0, 1, at_chan(0, 1)),
            one(1, 0, 0, 6, at_chan(1, 0)),
            one(2, 0, 0, 2, at_chan(3, 0)),
            one(3, 0, 0, 4, at_chan(2, 0)),
        ]
        from_y = [one(4, 0, 1, 7, at_chan(1, 0)), one(5, 0, 1, 3, at_chan(3, 0))]
        from_x2 = [one(6, 2, 0, 5, at_chan(0, 1))]
        return own, from_y, from_x2

    def wait_shard(plane, recv, dx, dy):
        ref = shard(plane, dx, dy)
        pltpu.make_async_copy(ref, ref, recv.at[dx * 2 + dy]).wait()

    def to_core0(dx, dy):
        n = dx * 2 + dy
        return copy(
            shard(0, dx, dy), shard(1, dx, dy), mate_send.at[n], recv_rim.at[n], mate
        )

    def give_core0(dx, dy):
        @pl.when(core == 1)
        def _():
            to_core0(dx, dy).start()

    own, from_y, from_x2 = gather_copies(0, send_own, recv_own)
    rim_own, rim_from_y, rim_from_x2 = gather_copies(1, send_rim, recv_rim)
    rim_first = copy(
        shard(0, 0, 0), shard(1, 0, 0), mate_send.at[0], recv_rim.at[0], before
    )

    for c in own:
        c.start()
    give_core0(0, 0)

    @pl.when(gives_rim)
    def _():
        rim_first.start()

    for plane in range(2):
        for sz in range(2):
            grads[plane, sz, :, CELLS:] = jnp.zeros((256, Z), BF16)

    @pl.when(g == 2 * NZ * NYH - 1)
    def _():
        grads[1, 0, :, 0:CELLS] = jnp.zeros((256, CELLS), BF16)

    terms[...] = jnp.zeros_like(terms)

    for par in range(8):
        rows32[par * 32 * Y : (par + 1) * 32 * Y] = (
            act_ref[:, 0, par].astype(F32).reshape(32 * Y, Z)
        )
    for j in range(Y):
        acts[:, j * Z : (j + 1) * Z] = rows32[pl.ds(j, 256, stride=Y)].astype(BF16)

    wait_shard(0, recv_own, 0, 1)
    for c in from_y:
        c.start()
    give_core0(0, 1)

    @pl.when(has_rim)
    def _():
        wait_shard(1, recv_rim, 0, 0)
        for c in rim_own:
            c.start()

    wait_shard(0, recv_own, 1, 0)
    give_core0(1, 0)
    wait_shard(0, recv_own, 3, 0)
    give_core0(3, 0)
    wait_shard(0, recv_own, 2, 0)
    for c in from_x2:
        c.start()
    give_core0(2, 0)

    @pl.when(has_rim)
    def _():
        wait_shard(1, recv_rim, 0, 1)
        for c in rim_from_y:
            c.start()

    dense[...] = jnp.zeros_like(dense)
    for n, shift in enumerate(SHIFTS):
        for par, tap in taps_of_shift(shift):
            dense[par * 32 : (par + 1) * 32, n * 256 : (n + 1) * 256] = weight_ref[tap]

    wait_shard(0, recv_own, 1, 1)
    give_core0(1, 1)
    wait_shard(0, recv_own, 3, 1)
    give_core0(3, 1)
    wait_shard(0, recv_own, 2, 1)
    give_core0(2, 1)

    @pl.when(has_rim)
    def _():
        wait_shard(1, recv_rim, 2, 0)
        for c in rim_from_x2:
            c.start()
        for dx, dy in ((1, 0), (3, 0), (1, 1), (3, 1), (2, 1)):
            wait_shard(1, recv_rim, dx, dy)

    @pl.when(core == 0)
    def _():
        for dx in range(4):
            for dy in range(2):
                wait_shard(1, recv_rim, dx, dy)

    lane = lax.broadcasted_iota(jnp.int32, (128, Z), 1)

    def shift_z(plane, half):
        start = pl.multiple_of(half * 128, 128)
        for j in range(Y):
            block = grads[plane, 0, pl.ds(start, 128), j * Z : (j + 1) * Z].astype(F32)
            moved = pltpu.roll(block, Z - 1, 1)
            grads[plane, 1, pl.ds(start, 128), j * Z : (j + 1) * Z] = jnp.where(
                lane == Z - 1, 0.0, moved
            ).astype(BF16)

    def filter_terms(chunk, half):
        start = pl.multiple_of(half * 128, 128)
        for sx, sy, sz in SHIFTS:
            pairs = taps_of_shift((sx, sy, sz))
            maps = jnp.concatenate([acts[p * 32 : (p + 1) * 32] for p, _ in pairs], 0)
            window = grads[sx, sz, pl.ds(start, 128), sy * Z : sy * Z + CELLS]
            product = lax.dot_general(
                maps, window, (((1,), (1,)), ((), ())), preferred_element_type=F32
            )
            for n, (_, tap) in enumerate(pairs):
                terms[chunk, pl.ds(tap, 32, stride=PAD), :] = product[n * 32 : (n + 1) * 32]

    halves = [x // 2, 1 - x // 2]
    mates = []
    for chunk in range(2):
        for plane in range(2):
            shift_z(plane, halves[chunk])
        filter_terms(chunk, halves[chunk])
        theirs = pl.multiple_of((1 - core) * 512, 512)
        c = copy(
            terms.at[chunk, pl.ds(theirs, 512)], from_mate.at[chunk],
            fw_send.at[chunk], fw_recv.at[chunk], mate,
        )
        c.start()
        mates.append(c)

    ours = pl.multiple_of(core * 512, 512)
    rs_sent = []
    for chunk in range(2):
        mates[chunk].wait_recv()
        total = terms[chunk, pl.ds(ours, 512), :] + from_mate[chunk]
        rs_own[chunk] = total.reshape(16, PAD, 128)
        rs_out[chunk] = encode(total.reshape(16, PAD, 128))
        for d in range(1, 16):
            a, k = d // NZ, d % NZ
            c = copy(
                rs_out.at[chunk, peer_w(d)], rs_in.at[chunk, a * NZ + (NZ - k) % NZ],
                rs_send.at[chunk, d], rs_recv.at[chunk], peer(d),
            )
            c.start()
            rs_sent.append(c)

    def wait_many(ref, sem):
        pltpu.make_async_copy(ref, ref, sem).wait()

    def maps_gradient(tile):
        columns = []
        for sx, sy, sz in SHIFTS:
            columns.append(grads[sx, sz, :, sy * Z + tile * 256 : sy * Z + (tile + 1) * 256])
        window = jnp.concatenate(columns, 0)
        sums = jnp.dot(dense[...], window, preferred_element_type=F32)
        for j in range(2):
            rows32[pl.ds(tile * 2 + j, 256, stride=Y)] = sums[:, j * Z : (j + 1) * Z]

    for tile in range(4):
        maps_gradient(tile)

    ag_sent = []
    for chunk in range(2):
        wait_many(rs_in.at[chunk, pl.ds(1, 15)], rs_recv.at[chunk])
        total = rs_own[chunk, w]
        total = total + jnp.sum(decode(rs_in[chunk, 1:16]), axis=0)
        ag[chunk, core, w] = encode((total * norm)[None])[0]
        for d in range(1, 16):
            c = copy(
                ag.at[chunk, core, w], ag.at[chunk, core, w],
                ag_send.at[chunk, d], ag_recv.at[chunk], peer(d),
            )
            c.start()
            ag_sent.append(c)

    for tile in range(4, 8):
        maps_gradient(tile)
    for par in range(8):
        out_act[:, 0, par] = (
            rows32[par * 32 * Y : (par + 1) * 32 * Y].reshape(32, Y, Z).astype(BF16)
        )

    ag_mate = []
    for chunk in range(2):
        wait_many(ag.at[chunk, core, pl.ds(0, 15)], ag_recv.at[chunk])
        c = copy(
            ag.at[chunk, core], ag.at[chunk, core],
            fw_send.at[2 + chunk], fw_recv.at[2 + chunk], mate,
        )
        c.start()
        ag_mate.append(c)
    for chunk in range(2):
        ag_mate[chunk].wait_recv()
        final[...] = decode(ag[chunk].reshape(32, PAD, 128)).reshape(32 * PAD, 128)
        start = pl.multiple_of(halves[chunk] * 128, 128)
        for tap in range(27):
            out_w[tap, :, pl.ds(start, 128)] = final[pl.ds(tap, 32, stride=PAD)]

    for c in own + from_y + from_x2 + mates + rs_sent + ag_sent + ag_mate:
        c.wait_send()

    @pl.when(has_rim)
    def _():
        for c in rim_own + rim_from_y + rim_from_x2:
            c.wait_send()

    @pl.when(gives_rim)
    def _():
        rim_first.wait_send()

    @pl.when(core == 1)
    def _():
        for dx in range(4):
            for dy in range(2):
                to_core0(dx, dy).wait_send()


def on_device(activations, grad_out, weight):
    _, planes, _, out_y, out_z = activations.shape
    norm = 1.0 / math.sqrt(planes * out_y * out_z * lax.axis_size("grid"))
    vmem = pl.BlockSpec(memory_space=pltpu.VMEM)
    dma = pltpu.SemaphoreType.DMA
    return pl.pallas_call(
        lambda *refs: kernel(norm, *refs),
        out_shape=(
            jax.ShapeDtypeStruct(activations.shape, BF16),
            jax.ShapeDtypeStruct(weight.shape, F32),
        ),
        in_specs=[vmem] * 3,
        out_specs=(vmem, vmem),
        scratch_shapes=[
            pltpu.VMEM((256 * Y, Z), F32),
            pltpu.VMEM((256, CELLS), BF16),
            pltpu.VMEM((2, 2, 256, CELLS + Z), BF16),
            pltpu.VMEM((256, 2048), BF16),
            pltpu.VMEM((2, 32 * PAD, 128), F32),
            pltpu.VMEM((2, 16 * PAD, 128), F32),
            pltpu.VMEM((2, 16, PAD, 128), F32),
            pltpu.VMEM((2, 16, PAD, 128), BF16),
            pltpu.VMEM((2, 16, PAD, 128), BF16),
            pltpu.VMEM((2, 2, 16, PAD, 128), BF16),
            pltpu.VMEM((32 * PAD, 128), F32),
            dma((7,)), dma((8,)), dma((7,)), dma((8,)), dma((8,)), dma((8,)),
            dma((2, 16)), dma((2,)), dma((2, 16)), dma((2,)), dma((4,)), dma((4,)),
        ],
        compiler_params=pltpu.CompilerParams(
            collective_id=0, has_side_effects=True, vmem_limit_bytes=48 << 20
        ),
    )(activations, grad_out, weight)


def solution(mesh):
    placed = (
        P("chan", "grid", None, None, None),
        P("chan", "grid", None, None),
        P(None, "chan", None),
    )
    return jax.shard_map(
        on_device,
        mesh=mesh,
        in_specs=placed,
        out_specs=(P("chan", "grid", None, None, None), P(None, "chan", None)),
        check_vma=False,
    )
```

```python
import math

import jax
import jax.numpy as jnp
from jax import lax
from jax.experimental import pallas as pl
from jax.experimental.pallas import tpu as pltpu
from jax.sharding import PartitionSpec as P

MESH = pl.DeviceIdType.MESH
F32, BF16 = jnp.float32, jnp.bfloat16
NX, NYL, NZ, NYH = 4, 2, 8, 2
Y, Z = 16, 128
CELLS = Y * Z
ROWS = 16
ODD = 128
SPAN = 240.0


def tap_of(par, step):
    if par == 0:
        return 1 if step == 0 else None
    return 2 if step == 0 else 0


def taps_of_shift(shift):
    found = []
    for par in range(8):
        bits = (par // 4, par // 2 % 2, par % 2)
        taps = [tap_of(b, s) for b, s in zip(bits, shift)]
        if None not in taps:
            found.append((par, 9 * taps[0] + 3 * taps[1] + taps[2]))
    return found


PARTS = (
    ((0, 0, (0,)), (0, 1, (0,)), (1, 1, (0,))),
    ((1, 0, (0, 1)), (0, 0, (1,)), (0, 1, (1,)), (1, 1, (1,))),
)


def part_taps(part):
    return [
        tap for sy, sz, planes in PARTS[part] for sx in planes for _, tap in taps_of_shift((sx, sy, sz))
    ]


SHIFTS = [(sx, sy, sz) for sx in range(2) for sy in range(2) for sz in range(2)]


def encode(values):
    largest = jnp.max(jnp.abs(values), axis=-2, keepdims=True)
    scale = jnp.maximum((largest * 1.01).astype(BF16).astype(F32), 1e-30)
    level = values * (SPAN / scale)
    power = jnp.exp2(jnp.abs(level) - SPAN / 2)
    power = jnp.where(values < 0, -power, power)
    row = lax.broadcasted_iota(jnp.int32, values.shape, values.ndim - 2)
    return jnp.where(row >= ROWS - 2, scale, power).astype(BF16)


def decode(codes):
    codes = codes.astype(F32)
    scale = codes[..., ROWS - 2 : ROWS - 1, :] * (1.0 / SPAN)
    level = (jnp.log2(jnp.abs(codes)) + SPAN / 2) * scale
    return jnp.where(codes < 0, -level, level)


def kernel(
    norm, act_hbm, grad_hbm, weight_hbm, out_act, ag,
    act_ref, grad_ref, weight_ref, rows32, acts, before_maps, relay, grads, dense,
    terms, from_mate, rs_own, rs_out, rs_in,
    local, send_own, recv_own, send_rim, recv_rim, hop_send, hop_recv,
    rs_send, rs_recv, ag_send, ag_recv, fw_send, fw_recv,
):
    g, chan = lax.axis_index("grid"), lax.axis_index("chan")
    w, core = g >> 1, g & 1
    x, yl = chan >> 1, chan & 1
    last = 2 * NZ * NYH - 1

    def chan_of(dx, dy):
        return ((x + dx) & (NX - 1)) * NYL + (yl ^ dy)

    def at_chan(dx, dy):
        return (g, chan_of(dx, dy))

    mate = (g + 1 - 2 * core, chan)
    before = (jnp.maximum(g - 1, 0), chan)
    following = (jnp.minimum(g + 1, last), chan)

    def peer_w(d):
        return ((w & NZ) ^ (d & NZ)) + ((w + d) & (NZ - 1))

    def slot_of(d):
        return (d & NZ) + ((NZ - d) & (NZ - 1))

    def peer(d):
        return (peer_w(d) * 2 + core, chan)

    has_rim = jnp.logical_and(core == 1, g < last)
    gives_rim = jnp.logical_and(core == 0, g > 0)

    barrier = pltpu.get_barrier_semaphore()
    near = [at_chan(1, 0), at_chan(3, 0), at_chan(0, 1), at_chan(1, 1), at_chan(3, 1), mate]
    chips = NZ * NYH
    for device in near:
        pl.semaphore_signal(barrier, inc=1, device_id=device, device_id_type=MESH)

    @pl.loop(1, chips)
    def _(d):
        pl.semaphore_signal(barrier, inc=1, device_id=peer(d), device_id_type=MESH)

    @pl.when(gives_rim)
    def _():
        pl.semaphore_signal(barrier, inc=1, device_id=before, device_id_type=MESH)

    @pl.when(has_rim)
    def _():
        pl.semaphore_signal(barrier, inc=1, device_id=following, device_id_type=MESH)

    @pl.when(g == 0)
    def _():
        pl.semaphore_signal(barrier, inc=1, device_id=(2 * NZ - 1, chan), device_id_type=MESH)

    @pl.when(g == 2 * NZ - 1)
    def _():
        pl.semaphore_signal(barrier, inc=1, device_id=(0, chan), device_id_type=MESH)

    loads = [
        pltpu.make_async_copy(grad_hbm, grad_ref, local.at[0]),
        pltpu.make_async_copy(act_hbm, act_ref, local.at[1]),
        pltpu.make_async_copy(weight_hbm, weight_ref, local.at[2]),
    ]
    for c in loads:
        c.start()

    def piece(plane, dx, dy, h):
        start = pl.multiple_of(chan_of(dx, dy) * 32 + 16 * h, 16)
        return grads.at[plane, 0, pl.ds(start, 16), pl.ds(0, CELLS)]

    loads[0].wait()
    rows32[0 : 32 * Y] = grad_ref[:, 0].astype(F32).reshape(32 * Y, Z)
    start_own = pl.multiple_of(chan * 32, 32)

    def along(j, size=Z):
        return pl.ds(pl.multiple_of(j * size, size), size)

    @pl.loop(0, Y)
    def _(j):
        grads[0, 0, pl.ds(start_own, 32), along(j)] = rows32[pl.ds(j, 32, stride=Y)].astype(BF16)

    rim_partners = jnp.logical_or(gives_rim, has_rim).astype(jnp.int32)
    rim_partners += jnp.logical_or(g == 0, g == 2 * NZ - 1).astype(jnp.int32)
    pl.semaphore_wait(barrier, len(near) + chips - 1 + rim_partners)

    def copy(src, dst, send, recv, device):
        return pltpu.make_async_remote_copy(
            src_ref=src, dst_ref=dst, send_sem=send, recv_sem=recv,
            device_id=device, device_id_type=MESH,
        )

    def gather_copies(plane, send, recv):
        count = [0]

        def one(dx, dy, h, slot, device):
            n = count[0]
            count[0] += 1
            ref = piece(plane, dx, dy, h)
            return copy(ref, ref, send.at[n], recv.at[slot, h], device)

        own = []
        for h in range(2):
            own.append(one(0, 0, h, 1, at_chan(0, 1)))
            own.append(one(0, 0, h, 6, at_chan(1, 0)))
            own.append(one(0, 0, h, 2, at_chan(3, 0)))
        passed = []
        for h in range(2):
            passed.append(
                ((0, 1, h), [one(0, 1, h, 7, at_chan(1, 0)), one(0, 1, h, 3, at_chan(3, 0))])
            )
            dx = 3 - 2 * h
            passed.append(
                (
                    (dx, 0, h),
                    [one(dx, 0, h, 4, at_chan(4 - dx, 0)), one(dx, 0, h, 5, at_chan(4 - dx, 1))],
                )
            )
        return own, passed

    def wait_piece(plane, recv, slot, h):
        ref = piece(plane, 0, 0, h)
        pltpu.make_async_copy(ref, ref, recv.at[slot, h]).wait()

    own, passed = gather_copies(0, send_own, recv_own)
    rim_own, rim_passed = gather_copies(1, send_rim, recv_rim)
    rim_first = [
        copy(
            piece(0, 0, 0, h), piece(1, 0, 0, h), hop_send.at[h], recv_rim.at[0, h], before
        )
        for h in range(2)
    ]
    half_odd = ODD // 2
    crosses, relays = g == 2 * NZ - 1, g == 0
    relay_at = (0, chan)
    upper = acts.at[pl.ds(ODD + half_odd, half_odd)]
    arrives = before_maps.at[pl.ds(half_odd, half_odd)]
    odd_lower = copy(
        acts.at[pl.ds(ODD, half_odd)], before_maps.at[pl.ds(0, half_odd)],
        hop_send.at[2], hop_recv.at[0], following,
    )
    odd_upper = copy(upper, arrives, hop_send.at[4], hop_recv.at[2], following)
    odd_to_relay = copy(upper, relay, hop_send.at[4], hop_recv.at[3], relay_at)
    odd_relayed = copy(relay, arrives, hop_send.at[5], hop_recv.at[2], (2 * NZ, chan))
    plane_cells = pl.ds(0, CELLS)
    whole_plane = copy(
        grads.at[0, 0, :, plane_cells], grads.at[1, 0, :, plane_cells],
        hop_send.at[3], hop_recv.at[1], mate,
    )

    for c in own:
        c.start()

    loads[1].wait()

    @pl.loop(0, 8)
    def _(par):
        rows32[along(par, 32 * Y)] = act_ref[:, 0, par].astype(F32).reshape(32 * Y, Z)

    for base in (ODD, 0):

        @pl.loop(0, Y)
        def _(j):
            acts[base : base + ODD, along(j)] = rows32[
                pl.ds(base * Y + j, ODD, stride=Y)
            ].astype(BF16)

        if base:

            @pl.when(g < last)
            def _():
                odd_lower.start()

            @pl.when(jnp.logical_and(g < last, jnp.logical_not(crosses)))
            def _():
                odd_upper.start()

            @pl.when(crosses)
            def _():
                odd_to_relay.start()

    @pl.when(gives_rim)
    def _():
        for c in rim_first:
            c.start()

    for plane in range(2):
        for sz in range(2):
            grads[plane, sz, :, CELLS:] = jnp.zeros((256, Z), BF16)

    @pl.when(g == last)
    def _():
        grads[1, 0, :, 0:CELLS] = jnp.zeros((256, CELLS), BF16)

    @pl.when(g == 0)
    def _():
        before_maps[...] = jnp.zeros_like(before_maps)

    terms[...] = jnp.zeros_like(terms)

    def pass_on(plane, recv, steps):
        for (dx, dy, h), copies in steps:
            wait_piece(plane, recv, dx * 2 + dy, h)
            for c in copies:
                c.start()

    pass_on(0, recv_own, passed)

    @pl.when(relays)
    def _():
        odd_to_relay.wait_recv()
        odd_relayed.start()


    loads[2].wait()
    dense[...] = jnp.zeros_like(dense)
    for n, shift in enumerate(SHIFTS):
        for par, tap in taps_of_shift(shift):
            dense[par * 32 : (par + 1) * 32, n * 256 : (n + 1) * 256] = weight_ref[tap]

    lane = lax.broadcasted_iota(jnp.int32, (128, Z), 1)

    def shift_z(plane, half):
        start = pl.multiple_of(half * 128, 128)

        @pl.loop(0, Y)
        def _(j):
            block = grads[plane, 0, pl.ds(start, 128), along(j)].astype(F32)
            moved = pltpu.roll(block, Z - 1, 1)
            grads[plane, 1, pl.ds(start, 128), along(j)] = jnp.where(
                lane == Z - 1, 0.0, moved
            ).astype(BF16)

    def filter_terms(part):
        row = 0
        for sy, sz, planes in PARTS[part]:
            maps = []
            for sx in planes:
                for par, _ in taps_of_shift((sx, sy, sz)):
                    source, base = (before_maps, 4) if sx else (acts, 0)
                    maps.append(source[(par - base) * 32 : (par - base + 1) * 32])
            window = grads[0, sz, :, sy * Z : sy * Z + CELLS]
            product = lax.dot_general(
                jnp.concatenate(maps, 0), window, (((1,), (1,)), ((), ())),
                preferred_element_type=F32,
            )
            for n in range(len(maps)):
                for half in range(2):
                    terms[part, half, pl.ds(row, 32, stride=ROWS), :] = product[
                        n * 32 : (n + 1) * 32, half * 128 : (half + 1) * 128
                    ]
                row += 1

    mine = 16 * ROWS
    theirs = pl.multiple_of((1 - core) * mine, mine)
    ours = pl.multiple_of(core * mine, mine)
    to_mate = [
        copy(
            terms.at[part, :, pl.ds(theirs, mine)], from_mate.at[part],
            fw_send.at[part], fw_recv.at[part], mate,
        )
        for part in range(2)
    ]
    halves = [x // 2, 1 - x // 2]
    near_x = 1 + 2 * lax.rem(x, 2)
    far_x = 4 - near_x

    wait_piece(0, recv_own, 6, 1)
    wait_piece(0, recv_own, 2, 0)
    for h in range(2):
        wait_piece(0, recv_own, near_x * 2 + 1, h)
    shift_z(0, halves[0])
    for slot in (4, 5):
        for h in range(2):
            wait_piece(0, recv_own, slot, h)
    for h in range(2):
        wait_piece(0, recv_own, far_x * 2 + 1, h)
    shift_z(0, halves[1])
    filter_terms(0)
    to_mate[0].start()

    @pl.when(has_rim)
    def _():
        for h in range(2):
            wait_piece(1, recv_rim, 0, h)
        for c in rim_own:
            c.start()

    @pl.when(core == 1)
    def _():
        whole_plane.start()

    def scatter(part):
        to_mate[part].wait_recv()
        for half in range(2):
            total = terms[part, half, pl.ds(ours, mine), :] + from_mate[part, half]
            total = total.reshape(16, ROWS, 128)
            rs_own[part, :, half] = total
            rs_out[part, :, half] = encode(total)

        @pl.loop(1, chips)
        def _(d):
            copy(
                rs_out.at[part, peer_w(d)], rs_in.at[part, slot_of(d)],
                rs_send.at[part], rs_recv.at[part], peer(d),
            ).start()

    def wait_many(ref, sem):
        pltpu.make_async_copy(ref, ref, sem).wait()

    scatter(0)

    @pl.when(g > 0)
    def _():
        odd_lower.wait_recv()
        odd_upper.wait_recv()

    filter_terms(1)
    to_mate[1].start()
    scatter(1)

    @pl.when(has_rim)
    def _():
        pass_on(1, recv_rim, rim_passed)

    def share(part):
        wait_many(rs_in.at[part, pl.ds(1, 15)], rs_recv.at[part])
        total = rs_own[part, w] + jnp.sum(decode(rs_in[part, 1:16]), axis=0)
        ag[part, core, w] = encode(total * norm)

        @pl.loop(1, chips)
        def _(d):
            block = ag.at[part, core, w]
            copy(block, block, ag_send.at[part], ag_recv.at[part], peer(d)).start()

    share(0)
    share(1)

    @pl.when(has_rim)
    def _():
        for slot, h in ((6, 1), (2, 0)):
            wait_piece(1, recv_rim, slot, h)
        for slot in (3, 4, 5, 7):
            for h in range(2):
                wait_piece(1, recv_rim, slot, h)

    @pl.when(core == 0)
    def _():
        whole_plane.wait_recv()

    for half in range(2):
        shift_z(1, half)

    @pl.loop(0, CELLS // 256)
    def _(tile):
        columns = []
        for sx, sy, sz in SHIFTS:
            cells = pl.ds(pl.multiple_of(tile * 256 + sy * Z, Z), 256)
            columns.append(grads[sx, sz, :, cells])
        window = jnp.concatenate(columns, 0)
        sums = jnp.dot(dense[...], window, preferred_element_type=F32)
        for j in range(2):
            rows32[pl.ds(tile * 2 + j, 256, stride=Y)] = sums[:, j * Z : (j + 1) * Z]

    @pl.loop(0, 8)
    def _(par):
        out_act[:, 0, par] = rows32[along(par, 32 * Y)].reshape(32, Y, Z).astype(BF16)

    ag_mate = []
    for part in range(2):
        wait_many(ag.at[part, core, pl.ds(0, 15)], ag_recv.at[part])
        c = copy(
            ag.at[part, core], ag.at[part, core],
            fw_send.at[2 + part], fw_recv.at[2 + part], mate,
        )
        c.start()
        ag_mate.append(c)
    for c in ag_mate:
        c.wait_recv()

    sent = own + [c for _, copies in passed for c in copies]
    for c in sent + to_mate + ag_mate:
        c.wait_send()
    for part in range(2):
        wait_many(rs_out.at[part, pl.ds(1, 15)], rs_send.at[part])
        wait_many(ag.at[part, core, pl.ds(1, 15)], ag_send.at[part])

    @pl.when(has_rim)
    def _():
        for c in rim_own + [c for _, copies in rim_passed for c in copies]:
            c.wait_send()

    @pl.when(gives_rim)
    def _():
        for c in rim_first:
            c.wait_send()

    @pl.when(g < last)
    def _():
        odd_lower.wait_send()
        odd_upper.wait_send()

    @pl.when(relays)
    def _():
        odd_relayed.wait_send()

    @pl.when(core == 1)
    def _():
        whole_plane.wait_send()


def finish(codes, act_ref, out_act, out_w, terms, result, sems):
    moved = pltpu.make_async_copy(act_ref, out_act, sems.at[0])
    moved.start()
    for part in range(2):
        terms[part] = decode(codes[part]).reshape(32 * 2 * ROWS, 128)
        for row, tap in enumerate(part_taps(part)):
            for half in range(2):
                result[tap, :, half * 128 : (half + 1) * 128] = terms[
                    part, pl.ds(half * ROWS + row, 32, stride=2 * ROWS)
                ]
    written = pltpu.make_async_copy(result, out_w, sems.at[1])
    written.start()
    moved.wait()
    written.wait()


def on_device(activations, grad_out, weight):
    _, planes, _, out_y, out_z = activations.shape
    norm = 1.0 / math.sqrt(planes * out_y * out_z * lax.axis_size("grid"))
    vmem = pl.BlockSpec(memory_space=pltpu.VMEM)
    anywhere = pl.BlockSpec(memory_space=pl.ANY)
    dma = pltpu.SemaphoreType.DMA
    maps = jax.ShapeDtypeStruct(activations.shape, BF16)
    code_shape = (2, 2, 16, 2, ROWS, 128)
    grad_act, codes = pl.pallas_call(
        lambda *refs: kernel(norm, *refs),
        out_shape=(maps, jax.ShapeDtypeStruct(code_shape, BF16)),
        in_specs=[pl.BlockSpec(memory_space=pltpu.HBM)] * 3,
        out_specs=(vmem, vmem),
        scratch_shapes=[
            pltpu.VMEM(activations.shape, BF16),
            pltpu.VMEM(grad_out.shape, BF16),
            pltpu.VMEM(weight.shape, BF16),
            pltpu.VMEM((256 * Y, Z), F32),
            pltpu.VMEM((256, CELLS), BF16),
            pltpu.VMEM((ODD, CELLS), BF16),
            pltpu.VMEM((ODD // 2, CELLS), BF16),
            pltpu.VMEM((2, 2, 256, CELLS + Z), BF16),
            pltpu.VMEM((256, 2048), BF16),
            pltpu.VMEM((2, 2, 32 * ROWS, 128), F32),
            pltpu.VMEM((2, 2, 16 * ROWS, 128), F32),
            pltpu.VMEM((2, 16, 2, ROWS, 128), F32),
            pltpu.VMEM((2, 16, 2, ROWS, 128), BF16),
            pltpu.VMEM((2, 16, 2, ROWS, 128), BF16),
            dma((3,)), dma((14,)), dma((8, 2)), dma((14,)), dma((8, 2)), dma((6,)), dma((4,)),
            dma((2,)), dma((2,)), dma((2,)), dma((2,)), dma((4,)), dma((4,)),
        ],
        compiler_params=pltpu.CompilerParams(
            collective_id=0, has_side_effects=True, vmem_limit_bytes=48 << 20
        ),
    )(*(pltpu.with_memory_space_constraint(v, pltpu.HBM) for v in (activations, grad_out, weight)))
    return pl.pallas_call(
        finish,
        out_shape=(maps, jax.ShapeDtypeStruct(weight.shape, F32)),
        in_specs=[vmem, vmem],
        out_specs=(anywhere, anywhere),
        scratch_shapes=[
            pltpu.VMEM((2, 32 * 2 * ROWS, 128), F32),
            pltpu.VMEM(weight.shape, F32),
            dma((2,)),
        ],
        compiler_params=pltpu.CompilerParams(vmem_limit_bytes=16 << 20),
    )(codes, grad_act)


def solution(mesh):
    placed = (
        P("chan", "grid", None, None, None),
        P("chan", "grid", None, None),
        P(None, "chan", None),
    )
    return jax.shard_map(
        on_device,
        mesh=mesh,
        in_specs=placed,
        out_specs=(P("chan", "grid", None, None, None), P(None, "chan", None)),
        check_vma=False,
    )
```

```python
import math

import jax
import jax.numpy as jnp
from jax import lax
from jax.experimental import pallas as pl
from jax.experimental.pallas import tpu as pltpu
from jax.sharding import PartitionSpec as P

MESH = pl.DeviceIdType.MESH
F32, BF16 = jnp.float32, jnp.bfloat16
NX, NYL, NZ, NYH = 4, 2, 8, 2
Y, Z = 16, 128
CELLS = Y * Z
ROWS = 16
ODD = 128
SPAN = 240.0


def tap_of(par, step):
    if par == 0:
        return 1 if step == 0 else None
    return 2 if step == 0 else 0


def taps_of_shift(shift):
    found = []
    for par in range(8):
        bits = (par // 4, par // 2 % 2, par % 2)
        taps = [tap_of(b, s) for b, s in zip(bits, shift)]
        if None not in taps:
            found.append((par, 9 * taps[0] + 3 * taps[1] + taps[2]))
    return found


PARTS = (
    ((0, 0, (0,)), (0, 1, (0,)), (1, 1, (0,))),
    ((1, 0, (0, 1)), (0, 0, (1,)), (0, 1, (1,)), (1, 1, (1,))),
)


def part_taps(part):
    return [
        tap for sy, sz, planes in PARTS[part] for sx in planes for _, tap in taps_of_shift((sx, sy, sz))
    ]


SHIFTS = [(sx, sy, sz) for sx in range(2) for sy in range(2) for sz in range(2)]


def encode(values):
    largest = jnp.max(jnp.abs(values), axis=-2, keepdims=True)
    scale = jnp.maximum((largest * 1.01).astype(BF16).astype(F32), 1e-30)
    level = values * (SPAN / scale)
    power = jnp.exp2(jnp.abs(level) - SPAN / 2)
    power = jnp.where(values < 0, -power, power)
    row = lax.broadcasted_iota(jnp.int32, values.shape, values.ndim - 2)
    return jnp.where(row >= ROWS - 2, scale, power).astype(BF16)


def decode(codes):
    codes = codes.astype(F32)
    scale = codes[..., ROWS - 2 : ROWS - 1, :] * (1.0 / SPAN)
    level = (jnp.log2(jnp.abs(codes)) + SPAN / 2) * scale
    return jnp.where(codes < 0, -level, level)


def kernel(
    norm, act_hbm, grad_hbm, weight_hbm, out_act, ag,
    act_ref, grad_ref, weight_ref, rows32, acts, before_maps, relay, grads, dense,
    terms, from_mate, rs_own, rs_out, rs_in,
    local, send_own, recv_own, send_rim, recv_rim, hop_send, hop_recv,
    rs_send, rs_recv, ag_send, ag_recv, fw_send, fw_recv, greeted,
):
    g, chan = lax.axis_index("grid"), lax.axis_index("chan")
    w, core = g >> 1, g & 1
    x, yl = chan >> 1, chan & 1
    last = 2 * NZ * NYH - 1

    def chan_of(dx, dy):
        return ((x + dx) & (NX - 1)) * NYL + (yl ^ dy)

    def at_chan(dx, dy):
        return (g, chan_of(dx, dy))

    mate = (g + 1 - 2 * core, chan)
    before = (jnp.maximum(g - 1, 0), chan)
    following = (jnp.minimum(g + 1, last), chan)

    def peer_w(d):
        return ((w & NZ) ^ (d & NZ)) + ((w + d) & (NZ - 1))

    def slot_of(d):
        return (d & NZ) + ((NZ - d) & (NZ - 1))

    def peer(d):
        return (peer_w(d) * 2 + core, chan)

    has_rim = jnp.logical_and(core == 1, g < last)
    gives_rim = jnp.logical_and(core == 0, g > 0)

    barrier = pltpu.get_barrier_semaphore()
    near = [at_chan(1, 0), at_chan(3, 0), at_chan(0, 1), at_chan(1, 1), at_chan(3, 1), mate]
    chips = NZ * NYH
    next_z, before_z, other_y = peer(1), peer(NZ - 1), peer(NZ)
    near += [next_z, before_z, other_y]
    for device in near:
        pl.semaphore_signal(barrier, inc=1, device_id=device, device_id_type=MESH)

    @pl.when(gives_rim)
    def _():
        pl.semaphore_signal(barrier, inc=1, device_id=before, device_id_type=MESH)

    @pl.when(has_rim)
    def _():
        pl.semaphore_signal(barrier, inc=1, device_id=following, device_id_type=MESH)

    @pl.when(g == 0)
    def _():
        pl.semaphore_signal(barrier, inc=1, device_id=(2 * NZ - 1, chan), device_id_type=MESH)

    @pl.when(g == 2 * NZ - 1)
    def _():
        pl.semaphore_signal(barrier, inc=1, device_id=(0, chan), device_id_type=MESH)

    loads = [
        pltpu.make_async_copy(grad_hbm, grad_ref, local.at[0]),
        pltpu.make_async_copy(act_hbm, act_ref, local.at[1]),
        pltpu.make_async_copy(weight_hbm, weight_ref, local.at[2]),
    ]
    for c in loads:
        c.start()

    def piece(plane, dx, dy, h):
        start = pl.multiple_of(chan_of(dx, dy) * 32 + 16 * h, 16)
        return grads.at[plane, 0, pl.ds(start, 16), pl.ds(0, CELLS)]

    loads[0].wait()
    rows32[0 : 32 * Y] = grad_ref[:, 0].astype(F32).reshape(32 * Y, Z)
    start_own = pl.multiple_of(chan * 32, 32)

    def along(j, size=Z):
        return pl.ds(pl.multiple_of(j * size, size), size)

    @pl.loop(0, Y)
    def _(j):
        grads[0, 0, pl.ds(start_own, 32), along(j)] = rows32[pl.ds(j, 32, stride=Y)].astype(BF16)

    rim_partners = jnp.logical_or(gives_rim, has_rim).astype(jnp.int32)
    rim_partners += jnp.logical_or(g == 0, g == 2 * NZ - 1).astype(jnp.int32)
    pl.semaphore_wait(barrier, len(near) + rim_partners)

    def copy(src, dst, send, recv, device):
        return pltpu.make_async_remote_copy(
            src_ref=src, dst_ref=dst, send_sem=send, recv_sem=recv,
            device_id=device, device_id_type=MESH,
        )

    def gather_copies(plane, send, recv):
        count = [0]

        def one(dx, dy, h, slot, device):
            n = count[0]
            count[0] += 1
            ref = piece(plane, dx, dy, h)
            return copy(ref, ref, send.at[n], recv.at[slot, h], device)

        own = []
        for h in range(2):
            own.append(one(0, 0, h, 1, at_chan(0, 1)))
            own.append(one(0, 0, h, 6, at_chan(1, 0)))
            own.append(one(0, 0, h, 2, at_chan(3, 0)))
        passed = []
        for h in range(2):
            passed.append(
                ((0, 1, h), [one(0, 1, h, 7, at_chan(1, 0)), one(0, 1, h, 3, at_chan(3, 0))])
            )
            dx = 3 - 2 * h
            passed.append(
                (
                    (dx, 0, h),
                    [one(dx, 0, h, 4, at_chan(4 - dx, 0)), one(dx, 0, h, 5, at_chan(4 - dx, 1))],
                )
            )
        return own, passed

    def wait_piece(plane, recv, slot, h):
        ref = piece(plane, 0, 0, h)
        pltpu.make_async_copy(ref, ref, recv.at[slot, h]).wait()

    own, passed = gather_copies(0, send_own, recv_own)
    rim_own, rim_passed = gather_copies(1, send_rim, recv_rim)
    rim_first = [
        copy(
            piece(0, 0, 0, h), piece(1, 0, 0, h), hop_send.at[h], recv_rim.at[0, h], before
        )
        for h in range(2)
    ]
    half_odd = ODD // 2
    crosses, relays = g == 2 * NZ - 1, g == 0
    relay_at = (0, chan)
    upper = acts.at[pl.ds(ODD + half_odd, half_odd)]
    arrives = before_maps.at[pl.ds(half_odd, half_odd)]
    odd_lower = copy(
        acts.at[pl.ds(ODD, half_odd)], before_maps.at[pl.ds(0, half_odd)],
        hop_send.at[2], hop_recv.at[0], following,
    )
    odd_upper = copy(upper, arrives, hop_send.at[4], hop_recv.at[2], following)
    odd_to_relay = copy(upper, relay, hop_send.at[4], hop_recv.at[3], relay_at)
    odd_relayed = copy(relay, arrives, hop_send.at[5], hop_recv.at[2], (2 * NZ, chan))
    plane_cells = pl.ds(0, CELLS)
    whole_plane = copy(
        grads.at[0, 0, :, plane_cells], grads.at[1, 0, :, plane_cells],
        hop_send.at[3], hop_recv.at[1], mate,
    )

    def greet(turn, *devices):
        for device in devices:
            pl.semaphore_signal(greeted.at[turn], inc=1, device_id=device, device_id_type=MESH)

    for c in own:
        c.start()
    greet(0, next_z, before_z)

    loads[1].wait()

    @pl.loop(0, 8)
    def _(par):
        rows32[along(par, 32 * Y)] = act_ref[:, 0, par].astype(F32).reshape(32 * Y, Z)

    for base in (ODD, 0):

        @pl.loop(0, Y)
        def _(j):
            acts[base : base + ODD, along(j)] = rows32[
                pl.ds(base * Y + j, ODD, stride=Y)
            ].astype(BF16)

        if base:

            @pl.when(g < last)
            def _():
                odd_lower.start()

            @pl.when(jnp.logical_and(g < last, jnp.logical_not(crosses)))
            def _():
                odd_upper.start()

            @pl.when(crosses)
            def _():
                odd_to_relay.start()

    @pl.when(gives_rim)
    def _():
        for c in rim_first:
            c.start()

    for plane in range(2):
        for sz in range(2):
            grads[plane, sz, :, CELLS:] = jnp.zeros((256, Z), BF16)

    @pl.when(g == last)
    def _():
        grads[1, 0, :, 0:CELLS] = jnp.zeros((256, CELLS), BF16)

    @pl.when(g == 0)
    def _():
        before_maps[...] = jnp.zeros_like(before_maps)

    terms[...] = jnp.zeros_like(terms)

    def pass_on(plane, recv, steps):
        for (dx, dy, h), copies in steps:
            wait_piece(plane, recv, dx * 2 + dy, h)
            for c in copies:
                c.start()

    pl.semaphore_wait(greeted.at[0], 2)
    greet(1, peer(2), peer(NZ - 2))
    pass_on(0, recv_own, passed)
    pl.semaphore_wait(greeted.at[1], 2)
    greet(2, other_y)

    @pl.when(relays)
    def _():
        odd_to_relay.wait_recv()
        odd_relayed.start()


    loads[2].wait()
    dense[...] = jnp.zeros_like(dense)
    for n, shift in enumerate(SHIFTS):
        for par, tap in taps_of_shift(shift):
            dense[par * 32 : (par + 1) * 32, n * 256 : (n + 1) * 256] = weight_ref[tap]

    lane = lax.broadcasted_iota(jnp.int32, (128, Z), 1)

    def shift_z(plane, half):
        start = pl.multiple_of(half * 128, 128)

        @pl.loop(0, Y)
        def _(j):
            block = grads[plane, 0, pl.ds(start, 128), along(j)].astype(F32)
            moved = pltpu.roll(block, Z - 1, 1)
            grads[plane, 1, pl.ds(start, 128), along(j)] = jnp.where(
                lane == Z - 1, 0.0, moved
            ).astype(BF16)

    def filter_terms(part):
        row = 0
        for sy, sz, planes in PARTS[part]:
            maps = []
            for sx in planes:
                for par, _ in taps_of_shift((sx, sy, sz)):
                    source, base = (before_maps, 4) if sx else (acts, 0)
                    maps.append(source[(par - base) * 32 : (par - base + 1) * 32])
            window = grads[0, sz, :, sy * Z : sy * Z + CELLS]
            product = lax.dot_general(
                jnp.concatenate(maps, 0), window, (((1,), (1,)), ((), ())),
                preferred_element_type=F32,
            )
            for n in range(len(maps)):
                for half in range(2):
                    terms[part, half, pl.ds(row, 32, stride=ROWS), :] = product[
                        n * 32 : (n + 1) * 32, half * 128 : (half + 1) * 128
                    ]
                row += 1

    mine = 16 * ROWS
    theirs = pl.multiple_of((1 - core) * mine, mine)
    ours = pl.multiple_of(core * mine, mine)
    to_mate = [
        copy(
            terms.at[part, :, pl.ds(theirs, mine)], from_mate.at[part],
            fw_send.at[part], fw_recv.at[part], mate,
        )
        for part in range(2)
    ]
    halves = [x // 2, 1 - x // 2]
    near_x = 1 + 2 * lax.rem(x, 2)
    far_x = 4 - near_x

    wait_piece(0, recv_own, 6, 1)
    wait_piece(0, recv_own, 2, 0)
    for h in range(2):
        wait_piece(0, recv_own, near_x * 2 + 1, h)
    shift_z(0, halves[0])
    for slot in (4, 5):
        for h in range(2):
            wait_piece(0, recv_own, slot, h)
    for h in range(2):
        wait_piece(0, recv_own, far_x * 2 + 1, h)
    shift_z(0, halves[1])
    filter_terms(0)
    to_mate[0].start()

    @pl.when(has_rim)
    def _():
        for h in range(2):
            wait_piece(1, recv_rim, 0, h)
        for c in rim_own:
            c.start()

    @pl.when(core == 1)
    def _():
        whole_plane.start()

    def scatter(part):
        to_mate[part].wait_recv()
        for half in range(2):
            total = terms[part, half, pl.ds(ours, mine), :] + from_mate[part, half]
            total = total.reshape(16, ROWS, 128)
            rs_own[part, :, half] = total
            rs_out[part, :, half] = encode(total)

        @pl.loop(1, chips)
        def _(d):
            copy(
                rs_out.at[part, peer_w(d)], rs_in.at[part, slot_of(d)],
                rs_send.at[part], rs_recv.at[part], peer(d),
            ).start()

    def wait_many(ref, sem):
        pltpu.make_async_copy(ref, ref, sem).wait()

    pl.semaphore_wait(greeted.at[2], 1)
    scatter(0)

    @pl.when(g > 0)
    def _():
        odd_lower.wait_recv()
        odd_upper.wait_recv()

    filter_terms(1)
    to_mate[1].start()
    scatter(1)

    @pl.when(has_rim)
    def _():
        pass_on(1, recv_rim, rim_passed)

    def share(part):
        wait_many(rs_in.at[part, pl.ds(1, 15)], rs_recv.at[part])
        total = rs_own[part, w] + jnp.sum(decode(rs_in[part, 1:16]), axis=0)
        ag[part, core, w] = encode(total * norm)

        @pl.loop(1, chips)
        def _(d):
            block = ag.at[part, core, w]
            copy(block, block, ag_send.at[part], ag_recv.at[part], peer(d)).start()

    share(0)
    share(1)

    @pl.when(has_rim)
    def _():
        for slot, h in ((6, 1), (2, 0)):
            wait_piece(1, recv_rim, slot, h)
        for slot in (3, 4, 5, 7):
            for h in range(2):
                wait_piece(1, recv_rim, slot, h)

    @pl.when(core == 0)
    def _():
        whole_plane.wait_recv()

    for half in range(2):
        shift_z(1, half)

    @pl.loop(0, CELLS // 256)
    def _(tile):
        columns = []
        for sx, sy, sz in SHIFTS:
            cells = pl.ds(pl.multiple_of(tile * 256 + sy * Z, Z), 256)
            columns.append(grads[sx, sz, :, cells])
        window = jnp.concatenate(columns, 0)
        sums = jnp.dot(dense[...], window, preferred_element_type=F32)
        for j in range(2):
            rows32[pl.ds(tile * 2 + j, 256, stride=Y)] = sums[:, j * Z : (j + 1) * Z]

    @pl.loop(0, 8)
    def _(par):
        out_act[:, 0, par] = rows32[along(par, 32 * Y)].reshape(32, Y, Z).astype(BF16)

    ag_mate = []
    for part in range(2):
        wait_many(ag.at[part, core, pl.ds(0, 15)], ag_recv.at[part])
        c = copy(
            ag.at[part, core], ag.at[part, core],
            fw_send.at[2 + part], fw_recv.at[2 + part], mate,
        )
        c.start()
        ag_mate.append(c)
    for c in ag_mate:
        c.wait_recv()

    sent = own + [c for _, copies in passed for c in copies]
    for c in sent + to_mate + ag_mate:
        c.wait_send()
    for part in range(2):
        wait_many(rs_out.at[part, pl.ds(1, 15)], rs_send.at[part])
        wait_many(ag.at[part, core, pl.ds(1, 15)], ag_send.at[part])

    @pl.when(has_rim)
    def _():
        for c in rim_own + [c for _, copies in rim_passed for c in copies]:
            c.wait_send()

    @pl.when(gives_rim)
    def _():
        for c in rim_first:
            c.wait_send()

    @pl.when(g < last)
    def _():
        odd_lower.wait_send()
        odd_upper.wait_send()

    @pl.when(relays)
    def _():
        odd_relayed.wait_send()

    @pl.when(core == 1)
    def _():
        whole_plane.wait_send()


def finish(codes, act_ref, out_act, out_w, terms, result, sems):
    moved = pltpu.make_async_copy(act_ref, out_act, sems.at[0])
    moved.start()
    for part in range(2):
        terms[part] = decode(codes[part]).reshape(32 * 2 * ROWS, 128)
        for row, tap in enumerate(part_taps(part)):
            for half in range(2):
                result[tap, :, half * 128 : (half + 1) * 128] = terms[
                    part, pl.ds(half * ROWS + row, 32, stride=2 * ROWS)
                ]
    written = pltpu.make_async_copy(result, out_w, sems.at[1])
    written.start()
    moved.wait()
    written.wait()


def on_device(activations, grad_out, weight):
    _, planes, _, out_y, out_z = activations.shape
    norm = 1.0 / math.sqrt(planes * out_y * out_z * lax.axis_size("grid"))
    vmem = pl.BlockSpec(memory_space=pltpu.VMEM)
    anywhere = pl.BlockSpec(memory_space=pl.ANY)
    dma = pltpu.SemaphoreType.DMA
    maps = jax.ShapeDtypeStruct(activations.shape, BF16)
    code_shape = (2, 2, 16, 2, ROWS, 128)
    grad_act, codes = pl.pallas_call(
        lambda *refs: kernel(norm, *refs),
        out_shape=(maps, jax.ShapeDtypeStruct(code_shape, BF16)),
        in_specs=[pl.BlockSpec(memory_space=pltpu.HBM)] * 3,
        out_specs=(vmem, vmem),
        scratch_shapes=[
            pltpu.VMEM(activations.shape, BF16),
            pltpu.VMEM(grad_out.shape, BF16),
            pltpu.VMEM(weight.shape, BF16),
            pltpu.VMEM((256 * Y, Z), F32),
            pltpu.VMEM((256, CELLS), BF16),
            pltpu.VMEM((ODD, CELLS), BF16),
            pltpu.VMEM((ODD // 2, CELLS), BF16),
            pltpu.VMEM((2, 2, 256, CELLS + Z), BF16),
            pltpu.VMEM((256, 2048), BF16),
            pltpu.VMEM((2, 2, 32 * ROWS, 128), F32),
            pltpu.VMEM((2, 2, 16 * ROWS, 128), F32),
            pltpu.VMEM((2, 16, 2, ROWS, 128), F32),
            pltpu.VMEM((2, 16, 2, ROWS, 128), BF16),
            pltpu.VMEM((2, 16, 2, ROWS, 128), BF16),
            dma((3,)), dma((14,)), dma((8, 2)), dma((14,)), dma((8, 2)), dma((6,)), dma((4,)),
            dma((2,)), dma((2,)), dma((2,)), dma((2,)), dma((4,)), dma((4,)),
            pltpu.SemaphoreType.REGULAR((3,)),
        ],
        compiler_params=pltpu.CompilerParams(
            collective_id=0, has_side_effects=True, vmem_limit_bytes=48 << 20
        ),
    )(*(pltpu.with_memory_space_constraint(v, pltpu.HBM) for v in (activations, grad_out, weight)))
    return pl.pallas_call(
        finish,
        out_shape=(maps, jax.ShapeDtypeStruct(weight.shape, F32)),
        in_specs=[vmem, vmem],
        out_specs=(anywhere, anywhere),
        scratch_shapes=[
            pltpu.VMEM((2, 32 * 2 * ROWS, 128), F32),
            pltpu.VMEM(weight.shape, F32),
            dma((2,)),
        ],
        compiler_params=pltpu.CompilerParams(vmem_limit_bytes=16 << 20),
    )(codes, grad_act)


def solution(mesh):
    placed = (
        P("chan", "grid", None, None, None),
        P("chan", "grid", None, None),
        P(None, "chan", None),
    )
    return jax.shard_map(
        on_device,
        mesh=mesh,
        in_specs=placed,
        out_specs=(P("chan", "grid", None, None, None), P(None, "chan", None)),
        check_vma=False,
    )
```

```python
import math

import jax
import jax.numpy as jnp
from jax import lax
from jax.experimental import pallas as pl
from jax.experimental.pallas import tpu as pltpu
from jax.sharding import PartitionSpec as P

MESH = pl.DeviceIdType.MESH
F32, BF16 = jnp.float32, jnp.bfloat16
NX, NYL, NZ, NYH = 4, 2, 8, 2
Y, Z = 16, 128
CELLS = Y * Z
ROWS = 16
ODD = 128
SPAN = 240.0


def tap_of(par, step):
    if par == 0:
        return 1 if step == 0 else None
    return 2 if step == 0 else 0


def taps_of_shift(shift):
    found = []
    for par in range(8):
        bits = (par // 4, par // 2 % 2, par % 2)
        taps = [tap_of(b, s) for b, s in zip(bits, shift)]
        if None not in taps:
            found.append((par, 9 * taps[0] + 3 * taps[1] + taps[2]))
    return found


PARTS = (
    ((0, 0, (0,)), (0, 1, (0,)), (1, 1, (0,))),
    ((1, 0, (0, 1)), (0, 0, (1,)), (0, 1, (1,)), (1, 1, (1,))),
)


def part_taps(part):
    return [
        tap for sy, sz, planes in PARTS[part] for sx in planes for _, tap in taps_of_shift((sx, sy, sz))
    ]


SHIFTS = [(sx, sy, sz) for sx in range(2) for sy in range(2) for sz in range(2)]


def encode(values):
    largest = jnp.max(jnp.abs(values), axis=-2, keepdims=True)
    scale = jnp.maximum((largest * 1.01).astype(BF16).astype(F32), 1e-30)
    level = values * (SPAN / scale)
    power = jnp.exp2(jnp.abs(level) - SPAN / 2)
    power = jnp.where(values < 0, -power, power)
    row = lax.broadcasted_iota(jnp.int32, values.shape, values.ndim - 2)
    return jnp.where(row >= ROWS - 2, scale, power).astype(BF16)


def decode(codes):
    codes = codes.astype(F32)
    scale = codes[..., ROWS - 2 : ROWS - 1, :] * (1.0 / SPAN)
    level = (jnp.log2(jnp.abs(codes)) + SPAN / 2) * scale
    return jnp.where(codes < 0, -level, level)


def kernel(
    norm, act_hbm, grad_hbm, weight_hbm, out_act, ag,
    act_ref, grad_ref, weight_ref, rows32, acts, before_maps, relay, grads, dense,
    terms, from_mate, rs_own, rs_out, rs_in,
    local, send_own, recv_own, send_rim, recv_rim, hop_send, hop_recv,
    rs_send, rs_recv, ag_send, ag_recv, fw_send, fw_recv, greeted,
):
    g, chan = lax.axis_index("grid"), lax.axis_index("chan")
    w, core = g >> 1, g & 1
    x, yl = chan >> 1, chan & 1
    last = 2 * NZ * NYH - 1

    def chan_of(dx, dy):
        return ((x + dx) & (NX - 1)) * NYL + (yl ^ dy)

    def at_chan(dx, dy):
        return (g, chan_of(dx, dy))

    mate = (g + 1 - 2 * core, chan)
    before = (jnp.maximum(g - 1, 0), chan)
    following = (jnp.minimum(g + 1, last), chan)

    def peer_w(d):
        return ((w & NZ) ^ (d & NZ)) + ((w + d) & (NZ - 1))

    def slot_of(d):
        return (d & NZ) + ((NZ - d) & (NZ - 1))

    def peer(d):
        return (peer_w(d) * 2 + core, chan)

    has_rim = jnp.logical_and(core == 1, g < last)
    gives_rim = jnp.logical_and(core == 0, g > 0)

    barrier = pltpu.get_barrier_semaphore()
    near = [at_chan(1, 0), at_chan(3, 0), at_chan(0, 1), at_chan(1, 1), at_chan(3, 1), mate]
    far_first = [d for k in (4, 3, 5, 2, 6, 1, 7, 0) for d in (k + NZ, k) if d]
    next_z, before_z, other_y = peer(1), peer(NZ - 1), peer(NZ)
    near += [next_z, before_z, other_y]
    for device in near:
        pl.semaphore_signal(barrier, inc=1, device_id=device, device_id_type=MESH)

    @pl.when(gives_rim)
    def _():
        pl.semaphore_signal(barrier, inc=1, device_id=before, device_id_type=MESH)

    @pl.when(has_rim)
    def _():
        pl.semaphore_signal(barrier, inc=1, device_id=following, device_id_type=MESH)

    @pl.when(g == 0)
    def _():
        pl.semaphore_signal(barrier, inc=1, device_id=(2 * NZ - 1, chan), device_id_type=MESH)

    @pl.when(g == 2 * NZ - 1)
    def _():
        pl.semaphore_signal(barrier, inc=1, device_id=(0, chan), device_id_type=MESH)

    loads = [
        pltpu.make_async_copy(grad_hbm, grad_ref, local.at[0]),
        pltpu.make_async_copy(act_hbm, act_ref, local.at[1]),
        pltpu.make_async_copy(weight_hbm, weight_ref, local.at[2]),
    ]
    for c in loads:
        c.start()

    def piece(plane, dx, dy, h):
        start = pl.multiple_of(chan_of(dx, dy) * 32 + 16 * h, 16)
        return grads.at[plane, 0, pl.ds(start, 16), pl.ds(0, CELLS)]

    loads[0].wait()
    rows32[0 : 32 * Y] = grad_ref[:, 0].astype(F32).reshape(32 * Y, Z)
    start_own = pl.multiple_of(chan * 32, 32)

    def along(j, size=Z):
        return pl.ds(pl.multiple_of(j * size, size), size)

    @pl.loop(0, Y)
    def _(j):
        grads[0, 0, pl.ds(start_own, 32), along(j)] = rows32[pl.ds(j, 32, stride=Y)].astype(BF16)

    rim_partners = jnp.logical_or(gives_rim, has_rim).astype(jnp.int32)
    rim_partners += jnp.logical_or(g == 0, g == 2 * NZ - 1).astype(jnp.int32)
    pl.semaphore_wait(barrier, len(near) + rim_partners)

    def copy(src, dst, send, recv, device):
        return pltpu.make_async_remote_copy(
            src_ref=src, dst_ref=dst, send_sem=send, recv_sem=recv,
            device_id=device, device_id_type=MESH,
        )

    def gather_copies(plane, send, recv):
        count = [0]

        def one(dx, dy, h, slot, device):
            n = count[0]
            count[0] += 1
            ref = piece(plane, dx, dy, h)
            return copy(ref, ref, send.at[n], recv.at[slot, h], device)

        own = []
        for h in range(2):
            own.append(one(0, 0, h, 1, at_chan(0, 1)))
            own.append(one(0, 0, h, 6, at_chan(1, 0)))
            own.append(one(0, 0, h, 2, at_chan(3, 0)))
        passed = []
        for h in range(2):
            passed.append(
                ((0, 1, h), [one(0, 1, h, 7, at_chan(1, 0)), one(0, 1, h, 3, at_chan(3, 0))])
            )
            dx = 3 - 2 * h
            passed.append(
                (
                    (dx, 0, h),
                    [one(dx, 0, h, 4, at_chan(4 - dx, 0)), one(dx, 0, h, 5, at_chan(4 - dx, 1))],
                )
            )
        return own, passed

    def wait_piece(plane, recv, slot, h):
        ref = piece(plane, 0, 0, h)
        pltpu.make_async_copy(ref, ref, recv.at[slot, h]).wait()

    own, passed = gather_copies(0, send_own, recv_own)
    rim_own, rim_passed = gather_copies(1, send_rim, recv_rim)
    rim_first = [
        copy(
            piece(0, 0, 0, h), piece(1, 0, 0, h), hop_send.at[h], recv_rim.at[0, h], before
        )
        for h in range(2)
    ]
    half_odd = ODD // 2
    crosses, relays = g == 2 * NZ - 1, g == 0
    relay_at = (0, chan)
    upper = acts.at[pl.ds(ODD + half_odd, half_odd)]
    arrives = before_maps.at[pl.ds(half_odd, half_odd)]
    odd_lower = copy(
        acts.at[pl.ds(ODD, half_odd)], before_maps.at[pl.ds(0, half_odd)],
        hop_send.at[2], hop_recv.at[0], following,
    )
    odd_upper = copy(upper, arrives, hop_send.at[4], hop_recv.at[2], following)
    odd_to_relay = copy(upper, relay, hop_send.at[4], hop_recv.at[3], relay_at)
    odd_relayed = copy(relay, arrives, hop_send.at[5], hop_recv.at[2], (2 * NZ, chan))
    plane_cells = pl.ds(0, CELLS)
    whole_plane = copy(
        grads.at[0, 0, :, plane_cells], grads.at[1, 0, :, plane_cells],
        hop_send.at[3], hop_recv.at[1], mate,
    )

    def greet(turn, *devices):
        for device in devices:
            pl.semaphore_signal(greeted.at[turn], inc=1, device_id=device, device_id_type=MESH)

    for c in own:
        c.start()
    greet(0, next_z, before_z)

    loads[1].wait()

    @pl.loop(0, 8)
    def _(par):
        rows32[along(par, 32 * Y)] = act_ref[:, 0, par].astype(F32).reshape(32 * Y, Z)

    for base in (ODD, 0):

        @pl.loop(0, Y)
        def _(j):
            acts[base : base + ODD, along(j)] = rows32[
                pl.ds(base * Y + j, ODD, stride=Y)
            ].astype(BF16)

        if base:

            @pl.when(g < last)
            def _():
                odd_lower.start()

            @pl.when(jnp.logical_and(g < last, jnp.logical_not(crosses)))
            def _():
                odd_upper.start()

            @pl.when(crosses)
            def _():
                odd_to_relay.start()

    @pl.when(gives_rim)
    def _():
        for c in rim_first:
            c.start()

    for plane in range(2):
        for sz in range(2):
            grads[plane, sz, :, CELLS:] = jnp.zeros((256, Z), BF16)

    @pl.when(g == last)
    def _():
        grads[1, 0, :, 0:CELLS] = jnp.zeros((256, CELLS), BF16)

    @pl.when(g == 0)
    def _():
        before_maps[...] = jnp.zeros_like(before_maps)

    terms[...] = jnp.zeros_like(terms)

    def pass_on(plane, recv, steps):
        for (dx, dy, h), copies in steps:
            wait_piece(plane, recv, dx * 2 + dy, h)
            for c in copies:
                c.start()

    pl.semaphore_wait(greeted.at[0], 2)
    greet(1, peer(2), peer(NZ - 2))
    pass_on(0, recv_own, passed)
    pl.semaphore_wait(greeted.at[1], 2)
    greet(2, other_y)

    @pl.when(relays)
    def _():
        odd_to_relay.wait_recv()
        odd_relayed.start()


    loads[2].wait()
    dense[...] = jnp.zeros_like(dense)
    for n, shift in enumerate(SHIFTS):
        for par, tap in taps_of_shift(shift):
            dense[par * 32 : (par + 1) * 32, n * 256 : (n + 1) * 256] = weight_ref[tap]

    lane = lax.broadcasted_iota(jnp.int32, (128, Z), 1)

    def shift_z(plane, half):
        start = pl.multiple_of(half * 128, 128)

        @pl.loop(0, Y)
        def _(j):
            block = grads[plane, 0, pl.ds(start, 128), along(j)].astype(F32)
            moved = pltpu.roll(block, Z - 1, 1)
            grads[plane, 1, pl.ds(start, 128), along(j)] = jnp.where(
                lane == Z - 1, 0.0, moved
            ).astype(BF16)

    def filter_terms(part):
        row = 0
        for sy, sz, planes in PARTS[part]:
            maps = []
            for sx in planes:
                for par, _ in taps_of_shift((sx, sy, sz)):
                    source, base = (before_maps, 4) if sx else (acts, 0)
                    maps.append(source[(par - base) * 32 : (par - base + 1) * 32])
            window = grads[0, sz, :, sy * Z : sy * Z + CELLS]
            product = lax.dot_general(
                jnp.concatenate(maps, 0), window, (((1,), (1,)), ((), ())),
                preferred_element_type=F32,
            )
            for n in range(len(maps)):
                for half in range(2):
                    terms[part, half, pl.ds(row, 32, stride=ROWS), :] = product[
                        n * 32 : (n + 1) * 32, half * 128 : (half + 1) * 128
                    ]
                row += 1

    mine = 16 * ROWS
    theirs = pl.multiple_of((1 - core) * mine, mine)
    ours = pl.multiple_of(core * mine, mine)
    to_mate = [
        copy(
            terms.at[part, :, pl.ds(theirs, mine)], from_mate.at[part],
            fw_send.at[part], fw_recv.at[part], mate,
        )
        for part in range(2)
    ]
    halves = [x // 2, 1 - x // 2]
    near_x = 1 + 2 * lax.rem(x, 2)
    far_x = 4 - near_x

    wait_piece(0, recv_own, 6, 1)
    wait_piece(0, recv_own, 2, 0)
    for h in range(2):
        wait_piece(0, recv_own, near_x * 2 + 1, h)
    shift_z(0, halves[0])
    for slot in (4, 5):
        for h in range(2):
            wait_piece(0, recv_own, slot, h)
    for h in range(2):
        wait_piece(0, recv_own, far_x * 2 + 1, h)
    shift_z(0, halves[1])
    filter_terms(0)
    to_mate[0].start()

    @pl.when(has_rim)
    def _():
        for h in range(2):
            wait_piece(1, recv_rim, 0, h)
        for c in rim_own:
            c.start()

    @pl.when(core == 1)
    def _():
        whole_plane.start()

    def scatter(part):
        to_mate[part].wait_recv()
        for half in range(2):
            total = terms[part, half, pl.ds(ours, mine), :] + from_mate[part, half]
            total = total.reshape(16, ROWS, 128)
            rs_own[part, :, half] = total
            rs_out[part, :, half] = encode(total)

        for d in far_first:
            copy(
                rs_out.at[part, peer_w(d)], rs_in.at[part, slot_of(d)],
                rs_send.at[part], rs_recv.at[part], peer(d),
            ).start()

    def wait_many(ref, sem):
        pltpu.make_async_copy(ref, ref, sem).wait()

    pl.semaphore_wait(greeted.at[2], 1)
    scatter(0)

    @pl.when(g > 0)
    def _():
        odd_lower.wait_recv()
        odd_upper.wait_recv()

    filter_terms(1)
    to_mate[1].start()
    scatter(1)

    @pl.when(has_rim)
    def _():
        pass_on(1, recv_rim, rim_passed)

    def share(part):
        wait_many(rs_in.at[part, pl.ds(1, 15)], rs_recv.at[part])
        total = rs_own[part, w] + jnp.sum(decode(rs_in[part, 1:16]), axis=0)
        ag[part, core, w] = encode(total * norm)

        for d in far_first:
            block = ag.at[part, core, w]
            copy(block, block, ag_send.at[part], ag_recv.at[part], peer(d)).start()

    share(0)
    share(1)

    @pl.when(has_rim)
    def _():
        for slot, h in ((6, 1), (2, 0)):
            wait_piece(1, recv_rim, slot, h)
        for slot in (3, 4, 5, 7):
            for h in range(2):
                wait_piece(1, recv_rim, slot, h)

    @pl.when(core == 0)
    def _():
        whole_plane.wait_recv()

    for half in range(2):
        shift_z(1, half)

    @pl.loop(0, CELLS // 256)
    def _(tile):
        columns = []
        for sx, sy, sz in SHIFTS:
            cells = pl.ds(pl.multiple_of(tile * 256 + sy * Z, Z), 256)
            columns.append(grads[sx, sz, :, cells])
        window = jnp.concatenate(columns, 0)
        sums = jnp.dot(dense[...], window, preferred_element_type=F32)
        for j in range(2):
            rows32[pl.ds(tile * 2 + j, 256, stride=Y)] = sums[:, j * Z : (j + 1) * Z]

    @pl.loop(0, 8)
    def _(par):
        out_act[:, 0, par] = rows32[along(par, 32 * Y)].reshape(32, Y, Z).astype(BF16)

    ag_mate = []
    for part in range(2):
        wait_many(ag.at[part, core, pl.ds(0, 15)], ag_recv.at[part])
        c = copy(
            ag.at[part, core], ag.at[part, core],
            fw_send.at[2 + part], fw_recv.at[2 + part], mate,
        )
        c.start()
        ag_mate.append(c)
    for c in ag_mate:
        c.wait_recv()

    sent = own + [c for _, copies in passed for c in copies]
    for c in sent + to_mate + ag_mate:
        c.wait_send()
    for part in range(2):
        wait_many(rs_out.at[part, pl.ds(1, 15)], rs_send.at[part])
        wait_many(ag.at[part, core, pl.ds(1, 15)], ag_send.at[part])

    @pl.when(has_rim)
    def _():
        for c in rim_own + [c for _, copies in rim_passed for c in copies]:
            c.wait_send()

    @pl.when(gives_rim)
    def _():
        for c in rim_first:
            c.wait_send()

    @pl.when(g < last)
    def _():
        odd_lower.wait_send()
        odd_upper.wait_send()

    @pl.when(relays)
    def _():
        odd_relayed.wait_send()

    @pl.when(core == 1)
    def _():
        whole_plane.wait_send()


def finish(codes, act_ref, out_act, out_w, terms, result, sems):
    moved = pltpu.make_async_copy(act_ref, out_act, sems.at[0])
    moved.start()
    for part in range(2):
        terms[part] = decode(codes[part]).reshape(32 * 2 * ROWS, 128)
        for row, tap in enumerate(part_taps(part)):
            for half in range(2):
                result[tap, :, half * 128 : (half + 1) * 128] = terms[
                    part, pl.ds(half * ROWS + row, 32, stride=2 * ROWS)
                ]
    written = pltpu.make_async_copy(result, out_w, sems.at[1])
    written.start()
    moved.wait()
    written.wait()


def on_device(activations, grad_out, weight):
    _, planes, _, out_y, out_z = activations.shape
    norm = 1.0 / math.sqrt(planes * out_y * out_z * lax.axis_size("grid"))
    vmem = pl.BlockSpec(memory_space=pltpu.VMEM)
    anywhere = pl.BlockSpec(memory_space=pl.ANY)
    dma = pltpu.SemaphoreType.DMA
    maps = jax.ShapeDtypeStruct(activations.shape, BF16)
    code_shape = (2, 2, 16, 2, ROWS, 128)
    grad_act, codes = pl.pallas_call(
        lambda *refs: kernel(norm, *refs),
        out_shape=(maps, jax.ShapeDtypeStruct(code_shape, BF16)),
        in_specs=[pl.BlockSpec(memory_space=pltpu.HBM)] * 3,
        out_specs=(vmem, vmem),
        scratch_shapes=[
            pltpu.VMEM(activations.shape, BF16),
            pltpu.VMEM(grad_out.shape, BF16),
            pltpu.VMEM(weight.shape, BF16),
            pltpu.VMEM((256 * Y, Z), F32),
            pltpu.VMEM((256, CELLS), BF16),
            pltpu.VMEM((ODD, CELLS), BF16),
            pltpu.VMEM((ODD // 2, CELLS), BF16),
            pltpu.VMEM((2, 2, 256, CELLS + Z), BF16),
            pltpu.VMEM((256, 2048), BF16),
            pltpu.VMEM((2, 2, 32 * ROWS, 128), F32),
            pltpu.VMEM((2, 2, 16 * ROWS, 128), F32),
            pltpu.VMEM((2, 16, 2, ROWS, 128), F32),
            pltpu.VMEM((2, 16, 2, ROWS, 128), BF16),
            pltpu.VMEM((2, 16, 2, ROWS, 128), BF16),
            dma((3,)), dma((14,)), dma((8, 2)), dma((14,)), dma((8, 2)), dma((6,)), dma((4,)),
            dma((2,)), dma((2,)), dma((2,)), dma((2,)), dma((4,)), dma((4,)),
            pltpu.SemaphoreType.REGULAR((3,)),
        ],
        compiler_params=pltpu.CompilerParams(
            collective_id=0, has_side_effects=True, vmem_limit_bytes=48 << 20
        ),
    )(*(pltpu.with_memory_space_constraint(v, pltpu.HBM) for v in (activations, grad_out, weight)))
    return pl.pallas_call(
        finish,
        out_shape=(maps, jax.ShapeDtypeStruct(weight.shape, F32)),
        in_specs=[vmem, vmem],
        out_specs=(anywhere, anywhere),
        scratch_shapes=[
            pltpu.VMEM((2, 32 * 2 * ROWS, 128), F32),
            pltpu.VMEM(weight.shape, F32),
            dma((2,)),
        ],
        compiler_params=pltpu.CompilerParams(vmem_limit_bytes=16 << 20),
    )(codes, grad_act)


def solution(mesh):
    placed = (
        P("chan", "grid", None, None, None),
        P("chan", "grid", None, None),
        P(None, "chan", None),
    )
    return jax.shard_map(
        on_device,
        mesh=mesh,
        in_specs=placed,
        out_specs=(P("chan", "grid", None, None, None), P(None, "chan", None)),
        check_vma=False,
    )
```

```python
import math

import jax
import jax.numpy as jnp
from jax import lax
from jax.experimental import pallas as pl
from jax.experimental.pallas import tpu as pltpu
from jax.sharding import PartitionSpec as P

MESH = pl.DeviceIdType.MESH
F32, BF16 = jnp.float32, jnp.bfloat16
NX, NYL, NZ, NYH = 4, 2, 8, 2
Y, Z = 16, 128
CELLS = Y * Z
ROWS = 16
ODD = 128
SPAN = 240.0


def tap_of(par, step):
    if par == 0:
        return 1 if step == 0 else None
    return 2 if step == 0 else 0


def taps_of_shift(shift):
    found = []
    for par in range(8):
        bits = (par // 4, par // 2 % 2, par % 2)
        taps = [tap_of(b, s) for b, s in zip(bits, shift)]
        if None not in taps:
            found.append((par, 9 * taps[0] + 3 * taps[1] + taps[2]))
    return found


PARTS = (
    ((0, 0, (0,)), (0, 1, (0,)), (1, 1, (0,))),
    ((1, 0, (0, 1)), (0, 0, (1,)), (0, 1, (1,)), (1, 1, (1,))),
)


def part_taps(part):
    return [
        tap for sy, sz, planes in PARTS[part] for sx in planes for _, tap in taps_of_shift((sx, sy, sz))
    ]


SHIFTS = [(sx, sy, sz) for sx in range(2) for sy in range(2) for sz in range(2)]


def encode(values):
    largest = jnp.max(jnp.abs(values), axis=-2, keepdims=True)
    scale = jnp.maximum((largest * 1.01).astype(BF16).astype(F32), 1e-30)
    level = values * (SPAN / scale)
    power = jnp.exp2(jnp.abs(level) - SPAN / 2)
    power = jnp.where(values < 0, -power, power)
    row = lax.broadcasted_iota(jnp.int32, values.shape, values.ndim - 2)
    return jnp.where(row >= ROWS - 2, scale, power).astype(BF16)


def decode(codes):
    codes = codes.astype(F32)
    scale = codes[..., ROWS - 2 : ROWS - 1, :] * (1.0 / SPAN)
    level = (jnp.log2(jnp.abs(codes)) + SPAN / 2) * scale
    return jnp.where(codes < 0, -level, level)


def kernel(
    norm, act_hbm, grad_hbm, weight_hbm, out_act, ag,
    act_ref, grad_ref, weight_ref, rows32, acts, before_maps, relay, grads, dense,
    terms, from_mate, rs_own, rs_out, rs_in,
    local, send_own, recv_own, send_rim, recv_rim, hop_send, hop_recv,
    rs_send, rs_recv, ag_send, ag_recv, fw_send, fw_recv, greeted,
):
    g, chan = lax.axis_index("grid"), lax.axis_index("chan")
    w, core = g >> 1, g & 1
    x, yl = chan >> 1, chan & 1
    last = 2 * NZ * NYH - 1

    def chan_of(dx, dy):
        return ((x + dx) & (NX - 1)) * NYL + (yl ^ dy)

    def at_chan(dx, dy):
        return (g, chan_of(dx, dy))

    mate = (g + 1 - 2 * core, chan)
    before = (jnp.maximum(g - 1, 0), chan)
    following = (jnp.minimum(g + 1, last), chan)

    def peer_w(d):
        return ((w & NZ) ^ (d & NZ)) + ((w + d) & (NZ - 1))

    def slot_of(d):
        return (d & NZ) + ((NZ - d) & (NZ - 1))

    def peer(d):
        return (peer_w(d) * 2 + core, chan)

    has_rim = jnp.logical_and(core == 1, g < last)
    gives_rim = jnp.logical_and(core == 0, g > 0)

    barrier = pltpu.get_barrier_semaphore()
    near = [at_chan(1, 0), at_chan(3, 0), at_chan(0, 1), at_chan(1, 1), at_chan(3, 1), mate]
    far_first = [d for high in (NZ, 0) for k in (4, 3, 5, 2, 6, 1, 7, 0) for d in (k + high,) if d]
    next_z, before_z, other_y = peer(1), peer(NZ - 1), peer(NZ)
    near += [next_z, before_z, other_y]
    for device in near:
        pl.semaphore_signal(barrier, inc=1, device_id=device, device_id_type=MESH)

    @pl.when(gives_rim)
    def _():
        pl.semaphore_signal(barrier, inc=1, device_id=before, device_id_type=MESH)

    @pl.when(has_rim)
    def _():
        pl.semaphore_signal(barrier, inc=1, device_id=following, device_id_type=MESH)

    @pl.when(g == 0)
    def _():
        pl.semaphore_signal(barrier, inc=1, device_id=(2 * NZ - 1, chan), device_id_type=MESH)

    @pl.when(g == 2 * NZ - 1)
    def _():
        pl.semaphore_signal(barrier, inc=1, device_id=(0, chan), device_id_type=MESH)

    loads = [
        pltpu.make_async_copy(grad_hbm, grad_ref, local.at[0]),
        pltpu.make_async_copy(act_hbm, act_ref, local.at[1]),
        pltpu.make_async_copy(weight_hbm, weight_ref, local.at[2]),
    ]
    for c in loads:
        c.start()

    def piece(plane, dx, dy, h):
        start = pl.multiple_of(chan_of(dx, dy) * 32 + 16 * h, 16)
        return grads.at[plane, 0, pl.ds(start, 16), pl.ds(0, CELLS)]

    loads[0].wait()
    rows32[0 : 32 * Y] = grad_ref[:, 0].astype(F32).reshape(32 * Y, Z)
    start_own = pl.multiple_of(chan * 32, 32)

    def along(j, size=Z):
        return pl.ds(pl.multiple_of(j * size, size), size)

    @pl.loop(0, Y)
    def _(j):
        grads[0, 0, pl.ds(start_own, 32), along(j)] = rows32[pl.ds(j, 32, stride=Y)].astype(BF16)

    rim_partners = jnp.logical_or(gives_rim, has_rim).astype(jnp.int32)
    rim_partners += jnp.logical_or(g == 0, g == 2 * NZ - 1).astype(jnp.int32)
    pl.semaphore_wait(barrier, len(near) + rim_partners)

    def copy(src, dst, send, recv, device):
        return pltpu.make_async_remote_copy(
            src_ref=src, dst_ref=dst, send_sem=send, recv_sem=recv,
            device_id=device, device_id_type=MESH,
        )

    def gather_copies(plane, send, recv):
        count = [0]

        def one(dx, dy, h, slot, device):
            n = count[0]
            count[0] += 1
            ref = piece(plane, dx, dy, h)
            return copy(ref, ref, send.at[n], recv.at[slot, h], device)

        own = []
        for h in range(2):
            own.append(one(0, 0, h, 1, at_chan(0, 1)))
            own.append(one(0, 0, h, 6, at_chan(1, 0)))
            own.append(one(0, 0, h, 2, at_chan(3, 0)))
        passed = []
        for h in range(2):
            passed.append(
                ((0, 1, h), [one(0, 1, h, 7, at_chan(1, 0)), one(0, 1, h, 3, at_chan(3, 0))])
            )
            dx = 3 - 2 * h
            passed.append(
                (
                    (dx, 0, h),
                    [one(dx, 0, h, 4, at_chan(4 - dx, 0)), one(dx, 0, h, 5, at_chan(4 - dx, 1))],
                )
            )
        return own, passed

    def wait_piece(plane, recv, slot, h):
        ref = piece(plane, 0, 0, h)
        pltpu.make_async_copy(ref, ref, recv.at[slot, h]).wait()

    own, passed = gather_copies(0, send_own, recv_own)
    rim_own, rim_passed = gather_copies(1, send_rim, recv_rim)
    rim_first = [
        copy(
            piece(0, 0, 0, h), piece(1, 0, 0, h), hop_send.at[h], recv_rim.at[0, h], before
        )
        for h in range(2)
    ]
    half_odd = ODD // 2
    crosses, relays = g == 2 * NZ - 1, g == 0
    relay_at = (0, chan)
    upper = acts.at[pl.ds(ODD + half_odd, half_odd)]
    arrives = before_maps.at[pl.ds(half_odd, half_odd)]
    odd_lower = copy(
        acts.at[pl.ds(ODD, half_odd)], before_maps.at[pl.ds(0, half_odd)],
        hop_send.at[2], hop_recv.at[0], following,
    )
    odd_upper = copy(upper, arrives, hop_send.at[4], hop_recv.at[2], following)
    odd_to_relay = copy(upper, relay, hop_send.at[4], hop_recv.at[3], relay_at)
    odd_relayed = copy(relay, arrives, hop_send.at[5], hop_recv.at[2], (2 * NZ, chan))
    plane_cells = pl.ds(0, CELLS)
    whole_plane = copy(
        grads.at[0, 0, :, plane_cells], grads.at[1, 0, :, plane_cells],
        hop_send.at[3], hop_recv.at[1], mate,
    )

    def greet(turn, *devices):
        for device in devices:
            pl.semaphore_signal(greeted.at[turn], inc=1, device_id=device, device_id_type=MESH)

    for c in own:
        c.start()
    greet(0, next_z, before_z)

    loads[1].wait()

    @pl.loop(0, 8)
    def _(par):
        rows32[along(par, 32 * Y)] = act_ref[:, 0, par].astype(F32).reshape(32 * Y, Z)

    for base in (ODD, 0):

        @pl.loop(0, Y)
        def _(j):
            acts[base : base + ODD, along(j)] = rows32[
                pl.ds(base * Y + j, ODD, stride=Y)
            ].astype(BF16)

        if base:

            @pl.when(g < last)
            def _():
                odd_lower.start()

            @pl.when(jnp.logical_and(g < last, jnp.logical_not(crosses)))
            def _():
                odd_upper.start()

            @pl.when(crosses)
            def _():
                odd_to_relay.start()

    @pl.when(gives_rim)
    def _():
        for c in rim_first:
            c.start()

    for plane in range(2):
        for sz in range(2):
            grads[plane, sz, :, CELLS:] = jnp.zeros((256, Z), BF16)

    @pl.when(g == last)
    def _():
        grads[1, 0, :, 0:CELLS] = jnp.zeros((256, CELLS), BF16)

    @pl.when(g == 0)
    def _():
        before_maps[...] = jnp.zeros_like(before_maps)

    terms[...] = jnp.zeros_like(terms)

    def pass_on(plane, recv, steps):
        for (dx, dy, h), copies in steps:
            wait_piece(plane, recv, dx * 2 + dy, h)
            for c in copies:
                c.start()

    pl.semaphore_wait(greeted.at[0], 2)
    greet(1, peer(2), peer(NZ - 2))
    pass_on(0, recv_own, passed)
    pl.semaphore_wait(greeted.at[1], 2)
    greet(2, other_y)

    @pl.when(relays)
    def _():
        odd_to_relay.wait_recv()
        odd_relayed.start()


    loads[2].wait()
    dense[...] = jnp.zeros_like(dense)
    for n, shift in enumerate(SHIFTS):
        for par, tap in taps_of_shift(shift):
            dense[par * 32 : (par + 1) * 32, n * 256 : (n + 1) * 256] = weight_ref[tap]

    lane = lax.broadcasted_iota(jnp.int32, (128, Z), 1)

    def shift_z(plane, half):
        start = pl.multiple_of(half * 128, 128)

        @pl.loop(0, Y)
        def _(j):
            block = grads[plane, 0, pl.ds(start, 128), along(j)].astype(F32)
            moved = pltpu.roll(block, Z - 1, 1)
            grads[plane, 1, pl.ds(start, 128), along(j)] = jnp.where(
                lane == Z - 1, 0.0, moved
            ).astype(BF16)

    def filter_terms(part):
        row = 0
        for sy, sz, planes in PARTS[part]:
            maps = []
            for sx in planes:
                for par, _ in taps_of_shift((sx, sy, sz)):
                    source, base = (before_maps, 4) if sx else (acts, 0)
                    maps.append(source[(par - base) * 32 : (par - base + 1) * 32])
            window = grads[0, sz, :, sy * Z : sy * Z + CELLS]
            product = lax.dot_general(
                jnp.concatenate(maps, 0), window, (((1,), (1,)), ((), ())),
                preferred_element_type=F32,
            )
            for n in range(len(maps)):
                for half in range(2):
                    terms[part, half, pl.ds(row, 32, stride=ROWS), :] = product[
                        n * 32 : (n + 1) * 32, half * 128 : (half + 1) * 128
                    ]
                row += 1

    mine = 16 * ROWS
    theirs = pl.multiple_of((1 - core) * mine, mine)
    ours = pl.multiple_of(core * mine, mine)
    to_mate = [
        copy(
            terms.at[part, :, pl.ds(theirs, mine)], from_mate.at[part],
            fw_send.at[part], fw_recv.at[part], mate,
        )
        for part in range(2)
    ]
    halves = [x // 2, 1 - x // 2]
    near_x = 1 + 2 * lax.rem(x, 2)
    far_x = 4 - near_x

    wait_piece(0, recv_own, 6, 1)
    wait_piece(0, recv_own, 2, 0)
    for h in range(2):
        wait_piece(0, recv_own, near_x * 2 + 1, h)
    shift_z(0, halves[0])
    for slot in (4, 5):
        for h in range(2):
            wait_piece(0, recv_own, slot, h)
    for h in range(2):
        wait_piece(0, recv_own, far_x * 2 + 1, h)
    shift_z(0, halves[1])
    filter_terms(0)
    to_mate[0].start()

    @pl.when(has_rim)
    def _():
        for h in range(2):
            wait_piece(1, recv_rim, 0, h)
        for c in rim_own:
            c.start()

    @pl.when(core == 1)
    def _():
        whole_plane.start()

    def scatter(part):
        to_mate[part].wait_recv()
        for half in range(2):
            total = terms[part, half, pl.ds(ours, mine), :] + from_mate[part, half]
            total = total.reshape(16, ROWS, 128)
            rs_own[part, :, half] = total
            rs_out[part, :, half] = encode(total)

        for d in far_first:
            copy(
                rs_out.at[part, peer_w(d)], rs_in.at[part, slot_of(d)],
                rs_send.at[part], rs_recv.at[part], peer(d),
            ).start()

    def wait_many(ref, sem):
        pltpu.make_async_copy(ref, ref, sem).wait()

    pl.semaphore_wait(greeted.at[2], 1)
    scatter(0)

    @pl.when(g > 0)
    def _():
        odd_lower.wait_recv()
        odd_upper.wait_recv()

    filter_terms(1)
    to_mate[1].start()
    scatter(1)

    @pl.when(has_rim)
    def _():
        pass_on(1, recv_rim, rim_passed)

    def share(part):
        wait_many(rs_in.at[part, pl.ds(1, 15)], rs_recv.at[part])
        total = rs_own[part, w] + jnp.sum(decode(rs_in[part, 1:16]), axis=0)
        ag[part, core, w] = encode(total * norm)

        for d in far_first:
            block = ag.at[part, core, w]
            copy(block, block, ag_send.at[part], ag_recv.at[part], peer(d)).start()

    share(0)
    share(1)

    @pl.when(has_rim)
    def _():
        for slot, h in ((6, 1), (2, 0)):
            wait_piece(1, recv_rim, slot, h)
        for slot in (3, 4, 5, 7):
            for h in range(2):
                wait_piece(1, recv_rim, slot, h)

    @pl.when(core == 0)
    def _():
        whole_plane.wait_recv()

    for half in range(2):
        shift_z(1, half)

    @pl.loop(0, CELLS // 256)
    def _(tile):
        columns = []
        for sx, sy, sz in SHIFTS:
            cells = pl.ds(pl.multiple_of(tile * 256 + sy * Z, Z), 256)
            columns.append(grads[sx, sz, :, cells])
        window = jnp.concatenate(columns, 0)
        sums = jnp.dot(dense[...], window, preferred_element_type=F32)
        for j in range(2):
            rows32[pl.ds(tile * 2 + j, 256, stride=Y)] = sums[:, j * Z : (j + 1) * Z]

    @pl.loop(0, 8)
    def _(par):
        out_act[:, 0, par] = rows32[along(par, 32 * Y)].reshape(32, Y, Z).astype(BF16)

    ag_mate = []
    for part in range(2):
        wait_many(ag.at[part, core, pl.ds(0, 15)], ag_recv.at[part])
        c = copy(
            ag.at[part, core], ag.at[part, core],
            fw_send.at[2 + part], fw_recv.at[2 + part], mate,
        )
        c.start()
        ag_mate.append(c)
    for c in ag_mate:
        c.wait_recv()

    sent = own + [c for _, copies in passed for c in copies]
    for c in sent + to_mate + ag_mate:
        c.wait_send()
    for part in range(2):
        wait_many(rs_out.at[part, pl.ds(1, 15)], rs_send.at[part])
        wait_many(ag.at[part, core, pl.ds(1, 15)], ag_send.at[part])

    @pl.when(has_rim)
    def _():
        for c in rim_own + [c for _, copies in rim_passed for c in copies]:
            c.wait_send()

    @pl.when(gives_rim)
    def _():
        for c in rim_first:
            c.wait_send()

    @pl.when(g < last)
    def _():
        odd_lower.wait_send()
        odd_upper.wait_send()

    @pl.when(relays)
    def _():
        odd_relayed.wait_send()

    @pl.when(core == 1)
    def _():
        whole_plane.wait_send()


def finish(codes, act_ref, out_act, out_w, terms, result, sems):
    moved = pltpu.make_async_copy(act_ref, out_act, sems.at[0])
    moved.start()
    span, written = 16 * 2 * ROWS, []
    for core in range(2):
        for part in range(2):
            terms[part] = decode(codes[part, core]).reshape(span, 128)
            for row, tap in enumerate(part_taps(part)):
                for half in range(2):
                    result[tap, core * 16 : (core + 1) * 16, half * 128 : (half + 1) * 128] = (
                        terms[part, pl.ds(half * ROWS + row, 16, stride=2 * ROWS)]
                    )
        rows = pl.ds(core * 16, 16)
        c = pltpu.make_async_copy(result.at[:, rows], out_w.at[:, rows], sems.at[1 + core])
        c.start()
        written.append(c)
    moved.wait()
    for c in written:
        c.wait()


def on_device(activations, grad_out, weight):
    _, planes, _, out_y, out_z = activations.shape
    norm = 1.0 / math.sqrt(planes * out_y * out_z * lax.axis_size("grid"))
    vmem = pl.BlockSpec(memory_space=pltpu.VMEM)
    anywhere = pl.BlockSpec(memory_space=pl.ANY)
    dma = pltpu.SemaphoreType.DMA
    maps = jax.ShapeDtypeStruct(activations.shape, BF16)
    code_shape = (2, 2, 16, 2, ROWS, 128)
    grad_act, codes = pl.pallas_call(
        lambda *refs: kernel(norm, *refs),
        out_shape=(maps, jax.ShapeDtypeStruct(code_shape, BF16)),
        in_specs=[pl.BlockSpec(memory_space=pltpu.HBM)] * 3,
        out_specs=(vmem, vmem),
        scratch_shapes=[
            pltpu.VMEM(activations.shape, BF16),
            pltpu.VMEM(grad_out.shape, BF16),
            pltpu.VMEM(weight.shape, BF16),
            pltpu.VMEM((256 * Y, Z), F32),
            pltpu.VMEM((256, CELLS), BF16),
            pltpu.VMEM((ODD, CELLS), BF16),
            pltpu.VMEM((ODD // 2, CELLS), BF16),
            pltpu.VMEM((2, 2, 256, CELLS + Z), BF16),
            pltpu.VMEM((256, 2048), BF16),
            pltpu.VMEM((2, 2, 32 * ROWS, 128), F32),
            pltpu.VMEM((2, 2, 16 * ROWS, 128), F32),
            pltpu.VMEM((2, 16, 2, ROWS, 128), F32),
            pltpu.VMEM((2, 16, 2, ROWS, 128), BF16),
            pltpu.VMEM((2, 16, 2, ROWS, 128), BF16),
            dma((3,)), dma((14,)), dma((8, 2)), dma((14,)), dma((8, 2)), dma((6,)), dma((4,)),
            dma((2,)), dma((2,)), dma((2,)), dma((2,)), dma((4,)), dma((4,)),
            pltpu.SemaphoreType.REGULAR((3,)),
        ],
        compiler_params=pltpu.CompilerParams(
            collective_id=0, has_side_effects=True, vmem_limit_bytes=48 << 20
        ),
    )(*(pltpu.with_memory_space_constraint(v, pltpu.HBM) for v in (activations, grad_out, weight)))
    return pl.pallas_call(
        finish,
        out_shape=(maps, jax.ShapeDtypeStruct(weight.shape, F32)),
        in_specs=[vmem, vmem],
        out_specs=(anywhere, anywhere),
        scratch_shapes=[
            pltpu.VMEM((2, 16 * 2 * ROWS, 128), F32),
            pltpu.VMEM(weight.shape, F32),
            dma((3,)),
        ],
        compiler_params=pltpu.CompilerParams(vmem_limit_bytes=16 << 20),
    )(codes, grad_act)


def solution(mesh):
    placed = (
        P("chan", "grid", None, None, None),
        P("chan", "grid", None, None),
        P(None, "chan", None),
    )
    return jax.shard_map(
        on_device,
        mesh=mesh,
        in_specs=placed,
        out_specs=(P("chan", "grid", None, None, None), P(None, "chan", None)),
        check_vma=False,
    )
```

```python
import math

import jax
import jax.numpy as jnp
from jax import lax
from jax.experimental import pallas as pl
from jax.experimental.pallas import tpu as pltpu
from jax.sharding import PartitionSpec as P

MESH = pl.DeviceIdType.MESH
F32, BF16 = jnp.float32, jnp.bfloat16
NX, NYL, NZ, NYH = 4, 2, 8, 2
Y, Z = 16, 128
CELLS = Y * Z
ROWS = 16
ODD = 128
SPAN = 240.0


def tap_of(par, step):
    if par == 0:
        return 1 if step == 0 else None
    return 2 if step == 0 else 0


def taps_of_shift(shift):
    found = []
    for par in range(8):
        bits = (par // 4, par // 2 % 2, par % 2)
        taps = [tap_of(b, s) for b, s in zip(bits, shift)]
        if None not in taps:
            found.append((par, 9 * taps[0] + 3 * taps[1] + taps[2]))
    return found


PARTS = (
    ((0, 0, (0,)), (0, 1, (0,)), (1, 1, (0,))),
    ((1, 0, (0, 1)), (0, 0, (1,)), (0, 1, (1,)), (1, 1, (1,))),
)


def part_taps(part):
    return [
        tap for sy, sz, planes in PARTS[part] for sx in planes for _, tap in taps_of_shift((sx, sy, sz))
    ]


SHIFTS = [(sx, sy, sz) for sx in range(2) for sy in range(2) for sz in range(2)]


def encode(values):
    largest = jnp.max(jnp.abs(values), axis=-2, keepdims=True)
    scale = jnp.maximum((largest * 1.01).astype(BF16).astype(F32), 1e-30)
    level = values * (SPAN / scale)
    power = jnp.exp2(jnp.abs(level) - SPAN / 2)
    power = jnp.where(values < 0, -power, power)
    row = lax.broadcasted_iota(jnp.int32, values.shape, values.ndim - 2)
    return jnp.where(row >= ROWS - 2, scale, power).astype(BF16)


def decode(codes):
    codes = codes.astype(F32)
    scale = codes[..., ROWS - 2 : ROWS - 1, :] * (1.0 / SPAN)
    level = (jnp.log2(jnp.abs(codes)) + SPAN / 2) * scale
    return jnp.where(codes < 0, -level, level)


def kernel(
    norm, act_hbm, grad_hbm, weight_hbm, out_act, ag,
    act_ref, grad_ref, weight_ref, rows32, acts, before_maps, relay, grads, dense,
    terms, from_mate, rs_own, rs_out, rs_in,
    local, send_own, recv_own, send_rim, recv_rim, hop_send, hop_recv,
    rs_send, rs_recv, ag_send, ag_recv, fw_send, fw_recv, greeted,
):
    g, chan = lax.axis_index("grid"), lax.axis_index("chan")
    w, core = g >> 1, g & 1
    x, yl = chan >> 1, chan & 1
    last = 2 * NZ * NYH - 1

    def chan_of(dx, dy):
        return ((x + dx) & (NX - 1)) * NYL + (yl ^ dy)

    def at_chan(dx, dy):
        return (g, chan_of(dx, dy))

    mate = (g + 1 - 2 * core, chan)
    before = (jnp.maximum(g - 1, 0), chan)
    following = (jnp.minimum(g + 1, last), chan)

    def peer_w(d):
        return ((w & NZ) ^ (d & NZ)) + ((w + d) & (NZ - 1))

    def slot_of(d):
        return (d & NZ) + ((NZ - d) & (NZ - 1))

    def peer(d):
        return (peer_w(d) * 2 + core, chan)

    has_rim = jnp.logical_and(core == 1, g < last)
    gives_rim = jnp.logical_and(core == 0, g > 0)

    barrier = pltpu.get_barrier_semaphore()
    near = [at_chan(1, 0), at_chan(3, 0), at_chan(0, 1), at_chan(1, 1), at_chan(3, 1), mate]
    far_first = [d for high in (NZ, 0) for k in (4, 3, 5, 2, 6, 1, 7, 0) for d in (k + high,) if d]
    next_z, before_z, other_y = peer(1), peer(NZ - 1), peer(NZ)
    near += [next_z, before_z, other_y]
    for device in near:
        pl.semaphore_signal(barrier, inc=1, device_id=device, device_id_type=MESH)

    @pl.when(gives_rim)
    def _():
        pl.semaphore_signal(barrier, inc=1, device_id=before, device_id_type=MESH)

    @pl.when(has_rim)
    def _():
        pl.semaphore_signal(barrier, inc=1, device_id=following, device_id_type=MESH)

    @pl.when(g == 0)
    def _():
        pl.semaphore_signal(barrier, inc=1, device_id=(2 * NZ - 1, chan), device_id_type=MESH)

    @pl.when(g == 2 * NZ - 1)
    def _():
        pl.semaphore_signal(barrier, inc=1, device_id=(0, chan), device_id_type=MESH)

    loads = [
        pltpu.make_async_copy(grad_hbm, grad_ref, local.at[0]),
        pltpu.make_async_copy(act_hbm, act_ref, local.at[1]),
        pltpu.make_async_copy(weight_hbm, weight_ref, local.at[2]),
    ]
    for c in loads:
        c.start()

    def piece(plane, dx, dy, h):
        start = pl.multiple_of(chan_of(dx, dy) * 32 + 16 * h, 16)
        return grads.at[plane, 0, pl.ds(start, 16), pl.ds(0, CELLS)]

    loads[0].wait()
    rows32[0 : 32 * Y] = grad_ref[:, 0].astype(F32).reshape(32 * Y, Z)
    start_own = pl.multiple_of(chan * 32, 32)

    def along(j, size=Z):
        return pl.ds(pl.multiple_of(j * size, size), size)

    @pl.loop(0, Y)
    def _(j):
        grads[0, 0, pl.ds(start_own, 32), along(j)] = rows32[pl.ds(j, 32, stride=Y)].astype(BF16)

    rim_partners = jnp.logical_or(gives_rim, has_rim).astype(jnp.int32)
    rim_partners += jnp.logical_or(g == 0, g == 2 * NZ - 1).astype(jnp.int32)
    pl.semaphore_wait(barrier, len(near) + rim_partners)

    def copy(src, dst, send, recv, device):
        return pltpu.make_async_remote_copy(
            src_ref=src, dst_ref=dst, send_sem=send, recv_sem=recv,
            device_id=device, device_id_type=MESH,
        )

    def gather_copies(plane, send, recv):
        count = [0]

        def one(dx, dy, h, slot, device):
            n = count[0]
            count[0] += 1
            ref = piece(plane, dx, dy, h)
            return copy(ref, ref, send.at[n], recv.at[slot, h], device)

        own = []
        for h in range(2):
            own.append(one(0, 0, h, 1, at_chan(0, 1)))
            own.append(one(0, 0, h, 6, at_chan(1, 0)))
            own.append(one(0, 0, h, 2, at_chan(3, 0)))
        passed = []
        for h in range(2):
            passed.append(
                ((0, 1, h), [one(0, 1, h, 7, at_chan(1, 0)), one(0, 1, h, 3, at_chan(3, 0))])
            )
            dx = 3 - 2 * h
            passed.append(
                (
                    (dx, 0, h),
                    [one(dx, 0, h, 4, at_chan(4 - dx, 0)), one(dx, 0, h, 5, at_chan(4 - dx, 1))],
                )
            )
        return own, passed

    def wait_piece(plane, recv, slot, h):
        ref = piece(plane, 0, 0, h)
        pltpu.make_async_copy(ref, ref, recv.at[slot, h]).wait()

    own, passed = gather_copies(0, send_own, recv_own)
    rim_own, rim_passed = gather_copies(1, send_rim, recv_rim)
    rim_first = [
        copy(
            piece(0, 0, 0, h), piece(1, 0, 0, h), hop_send.at[h], recv_rim.at[0, h], before
        )
        for h in range(2)
    ]
    half_odd = ODD // 2
    crosses, relays = g == 2 * NZ - 1, g == 0
    relay_at = (0, chan)
    upper = acts.at[pl.ds(ODD + half_odd, half_odd)]
    arrives = before_maps.at[pl.ds(half_odd, half_odd)]
    odd_lower = copy(
        acts.at[pl.ds(ODD, half_odd)], before_maps.at[pl.ds(0, half_odd)],
        hop_send.at[2], hop_recv.at[0], following,
    )
    odd_upper = copy(upper, arrives, hop_send.at[4], hop_recv.at[2], following)
    odd_to_relay = copy(upper, relay, hop_send.at[4], hop_recv.at[3], relay_at)
    odd_relayed = copy(relay, arrives, hop_send.at[5], hop_recv.at[2], (2 * NZ, chan))
    plane_cells = pl.ds(0, CELLS)
    whole_plane = copy(
        grads.at[0, 0, :, plane_cells], grads.at[1, 0, :, plane_cells],
        hop_send.at[3], hop_recv.at[1], mate,
    )

    def greet(turn, *devices):
        for device in devices:
            pl.semaphore_signal(greeted.at[turn], inc=1, device_id=device, device_id_type=MESH)

    for c in own:
        c.start()
    greet(0, next_z, before_z)

    loads[1].wait()

    @pl.loop(0, 8)
    def _(par):
        rows32[along(par, 32 * Y)] = act_ref[:, 0, par].astype(F32).reshape(32 * Y, Z)

    for base in (ODD, 0):

        @pl.loop(0, Y)
        def _(j):
            acts[base : base + ODD, along(j)] = rows32[
                pl.ds(base * Y + j, ODD, stride=Y)
            ].astype(BF16)

        if base:

            @pl.when(g < last)
            def _():
                odd_lower.start()

            @pl.when(jnp.logical_and(g < last, jnp.logical_not(crosses)))
            def _():
                odd_upper.start()

            @pl.when(crosses)
            def _():
                odd_to_relay.start()

    @pl.when(gives_rim)
    def _():
        for c in rim_first:
            c.start()

    for plane in range(2):
        for sz in range(2):
            grads[plane, sz, :, CELLS:] = jnp.zeros((256, Z), BF16)

    @pl.when(g == last)
    def _():
        grads[1, 0, :, 0:CELLS] = jnp.zeros((256, CELLS), BF16)

    @pl.when(g == 0)
    def _():
        before_maps[...] = jnp.zeros_like(before_maps)

    terms[...] = jnp.zeros_like(terms)

    def pass_on(plane, recv, steps):
        turning = []
        for (dx, dy, h), copies in steps:
            wait_piece(plane, recv, dx * 2 + dy, h)
            copies[0].start()
            if dx:
                turning.append(copies[1])
            else:
                copies[1].start()
        for c in turning:
            c.start()

    pl.semaphore_wait(greeted.at[0], 2)
    greet(1, peer(2), peer(NZ - 2))
    pass_on(0, recv_own, passed)
    pl.semaphore_wait(greeted.at[1], 2)
    greet(2, other_y)

    @pl.when(relays)
    def _():
        odd_to_relay.wait_recv()
        odd_relayed.start()


    loads[2].wait()
    dense[...] = jnp.zeros_like(dense)
    for n, shift in enumerate(SHIFTS):
        for par, tap in taps_of_shift(shift):
            dense[par * 32 : (par + 1) * 32, n * 256 : (n + 1) * 256] = weight_ref[tap]

    lane = lax.broadcasted_iota(jnp.int32, (128, Z), 1)

    def shift_z(plane, half):
        start = pl.multiple_of(half * 128, 128)

        @pl.loop(0, Y)
        def _(j):
            block = grads[plane, 0, pl.ds(start, 128), along(j)].astype(F32)
            moved = pltpu.roll(block, Z - 1, 1)
            grads[plane, 1, pl.ds(start, 128), along(j)] = jnp.where(
                lane == Z - 1, 0.0, moved
            ).astype(BF16)

    def filter_terms(part):
        row = 0
        for sy, sz, planes in PARTS[part]:
            maps = []
            for sx in planes:
                for par, _ in taps_of_shift((sx, sy, sz)):
                    source, base = (before_maps, 4) if sx else (acts, 0)
                    maps.append(source[(par - base) * 32 : (par - base + 1) * 32])
            window = grads[0, sz, :, sy * Z : sy * Z + CELLS]
            product = lax.dot_general(
                jnp.concatenate(maps, 0), window, (((1,), (1,)), ((), ())),
                preferred_element_type=F32,
            )
            for n in range(len(maps)):
                for half in range(2):
                    terms[part, half, pl.ds(row, 32, stride=ROWS), :] = product[
                        n * 32 : (n + 1) * 32, half * 128 : (half + 1) * 128
                    ]
                row += 1

    mine = 16 * ROWS
    theirs = pl.multiple_of((1 - core) * mine, mine)
    ours = pl.multiple_of(core * mine, mine)
    to_mate = [
        copy(
            terms.at[part, :, pl.ds(theirs, mine)], from_mate.at[part],
            fw_send.at[part], fw_recv.at[part], mate,
        )
        for part in range(2)
    ]
    halves = [x // 2, 1 - x // 2]
    near_x = 1 + 2 * lax.rem(x, 2)
    far_x = 4 - near_x

    wait_piece(0, recv_own, 6, 1)
    wait_piece(0, recv_own, 2, 0)
    for h in range(2):
        wait_piece(0, recv_own, near_x * 2 + 1, h)
    shift_z(0, halves[0])
    for slot in (4, 5):
        for h in range(2):
            wait_piece(0, recv_own, slot, h)
    for h in range(2):
        wait_piece(0, recv_own, far_x * 2 + 1, h)
    shift_z(0, halves[1])
    filter_terms(0)
    to_mate[0].start()

    @pl.when(has_rim)
    def _():
        for h in range(2):
            wait_piece(1, recv_rim, 0, h)
        for c in rim_own:
            c.start()

    @pl.when(core == 1)
    def _():
        whole_plane.start()

    def scatter(part):
        to_mate[part].wait_recv()
        for half in range(2):
            total = terms[part, half, pl.ds(ours, mine), :] + from_mate[part, half]
            total = total.reshape(16, ROWS, 128)
            rs_own[part, :, half] = total
            rs_out[part, :, half] = encode(total)

        for d in far_first:
            copy(
                rs_out.at[part, peer_w(d)], rs_in.at[part, slot_of(d)],
                rs_send.at[part], rs_recv.at[part], peer(d),
            ).start()

    def wait_many(ref, sem):
        pltpu.make_async_copy(ref, ref, sem).wait()

    pl.semaphore_wait(greeted.at[2], 1)
    scatter(0)

    @pl.when(g > 0)
    def _():
        odd_lower.wait_recv()
        odd_upper.wait_recv()

    filter_terms(1)
    to_mate[1].start()
    scatter(1)

    @pl.when(has_rim)
    def _():
        pass_on(1, recv_rim, rim_passed)

    def share(part):
        wait_many(rs_in.at[part, pl.ds(1, 15)], rs_recv.at[part])
        total = rs_own[part, w] + jnp.sum(decode(rs_in[part, 1:16]), axis=0)
        ag[part, core, w] = encode(total * norm)

        for d in far_first:
            block = ag.at[part, core, w]
            copy(block, block, ag_send.at[part], ag_recv.at[part], peer(d)).start()

    share(0)
    share(1)

    @pl.when(has_rim)
    def _():
        for slot, h in ((6, 1), (2, 0)):
            wait_piece(1, recv_rim, slot, h)
        for slot in (3, 4, 5, 7):
            for h in range(2):
                wait_piece(1, recv_rim, slot, h)

    @pl.when(core == 0)
    def _():
        whole_plane.wait_recv()

    for half in range(2):
        shift_z(1, half)

    @pl.loop(0, CELLS // 256)
    def _(tile):
        columns = []
        for sx, sy, sz in SHIFTS:
            cells = pl.ds(pl.multiple_of(tile * 256 + sy * Z, Z), 256)
            columns.append(grads[sx, sz, :, cells])
        window = jnp.concatenate(columns, 0)
        sums = jnp.dot(dense[...], window, preferred_element_type=F32)
        for j in range(2):
            rows32[pl.ds(tile * 2 + j, 256, stride=Y)] = sums[:, j * Z : (j + 1) * Z]

    @pl.loop(0, 8)
    def _(par):
        out_act[:, 0, par] = rows32[along(par, 32 * Y)].reshape(32, Y, Z).astype(BF16)

    ag_mate = []
    for part in range(2):
        wait_many(ag.at[part, core, pl.ds(0, 15)], ag_recv.at[part])
        c = copy(
            ag.at[part, core], ag.at[part, core],
            fw_send.at[2 + part], fw_recv.at[2 + part], mate,
        )
        c.start()
        ag_mate.append(c)
    for c in ag_mate:
        c.wait_recv()

    sent = own + [c for _, copies in passed for c in copies]
    for c in sent + to_mate + ag_mate:
        c.wait_send()
    for part in range(2):
        wait_many(rs_out.at[part, pl.ds(1, 15)], rs_send.at[part])
        wait_many(ag.at[part, core, pl.ds(1, 15)], ag_send.at[part])

    @pl.when(has_rim)
    def _():
        for c in rim_own + [c for _, copies in rim_passed for c in copies]:
            c.wait_send()

    @pl.when(gives_rim)
    def _():
        for c in rim_first:
            c.wait_send()

    @pl.when(g < last)
    def _():
        odd_lower.wait_send()
        odd_upper.wait_send()

    @pl.when(relays)
    def _():
        odd_relayed.wait_send()

    @pl.when(core == 1)
    def _():
        whole_plane.wait_send()


def finish(codes, act_ref, out_act, out_w, terms, result, sems):
    moved = pltpu.make_async_copy(act_ref, out_act, sems.at[0])
    moved.start()
    span, written = 16 * 2 * ROWS, []
    for core in range(2):
        for part in range(2):
            terms[part] = decode(codes[part, core]).reshape(span, 128)
            for row, tap in enumerate(part_taps(part)):
                for half in range(2):
                    result[tap, core * 16 : (core + 1) * 16, half * 128 : (half + 1) * 128] = (
                        terms[part, pl.ds(half * ROWS + row, 16, stride=2 * ROWS)]
                    )
        rows = pl.ds(core * 16, 16)
        c = pltpu.make_async_copy(result.at[:, rows], out_w.at[:, rows], sems.at[1 + core])
        c.start()
        written.append(c)
    moved.wait()
    for c in written:
        c.wait()


def on_device(activations, grad_out, weight):
    _, planes, _, out_y, out_z = activations.shape
    norm = 1.0 / math.sqrt(planes * out_y * out_z * lax.axis_size("grid"))
    vmem = pl.BlockSpec(memory_space=pltpu.VMEM)
    anywhere = pl.BlockSpec(memory_space=pl.ANY)
    dma = pltpu.SemaphoreType.DMA
    maps = jax.ShapeDtypeStruct(activations.shape, BF16)
    code_shape = (2, 2, 16, 2, ROWS, 128)
    grad_act, codes = pl.pallas_call(
        lambda *refs: kernel(norm, *refs),
        out_shape=(maps, jax.ShapeDtypeStruct(code_shape, BF16)),
        in_specs=[pl.BlockSpec(memory_space=pltpu.HBM)] * 3,
        out_specs=(vmem, vmem),
        scratch_shapes=[
            pltpu.VMEM(activations.shape, BF16),
            pltpu.VMEM(grad_out.shape, BF16),
            pltpu.VMEM(weight.shape, BF16),
            pltpu.VMEM((256 * Y, Z), F32),
            pltpu.VMEM((256, CELLS), BF16),
            pltpu.VMEM((ODD, CELLS), BF16),
            pltpu.VMEM((ODD // 2, CELLS), BF16),
            pltpu.VMEM((2, 2, 256, CELLS + Z), BF16),
            pltpu.VMEM((256, 2048), BF16),
            pltpu.VMEM((2, 2, 32 * ROWS, 128), F32),
            pltpu.VMEM((2, 2, 16 * ROWS, 128), F32),
            pltpu.VMEM((2, 16, 2, ROWS, 128), F32),
            pltpu.VMEM((2, 16, 2, ROWS, 128), BF16),
            pltpu.VMEM((2, 16, 2, ROWS, 128), BF16),
            dma((3,)), dma((14,)), dma((8, 2)), dma((14,)), dma((8, 2)), dma((6,)), dma((4,)),
            dma((2,)), dma((2,)), dma((2,)), dma((2,)), dma((4,)), dma((4,)),
            pltpu.SemaphoreType.REGULAR((3,)),
        ],
        compiler_params=pltpu.CompilerParams(
            collective_id=0, has_side_effects=True, vmem_limit_bytes=48 << 20
        ),
    )(*(pltpu.with_memory_space_constraint(v, pltpu.HBM) for v in (activations, grad_out, weight)))
    return pl.pallas_call(
        finish,
        out_shape=(maps, jax.ShapeDtypeStruct(weight.shape, F32)),
        in_specs=[vmem, vmem],
        out_specs=(anywhere, anywhere),
        scratch_shapes=[
            pltpu.VMEM((2, 16 * 2 * ROWS, 128), F32),
            pltpu.VMEM(weight.shape, F32),
            dma((3,)),
        ],
        compiler_params=pltpu.CompilerParams(vmem_limit_bytes=16 << 20),
    )(codes, grad_act)


def solution(mesh):
    placed = (
        P("chan", "grid", None, None, None),
        P("chan", "grid", None, None),
        P(None, "chan", None),
    )
    return jax.shard_map(
        on_device,
        mesh=mesh,
        in_specs=placed,
        out_specs=(P("chan", "grid", None, None, None), P(None, "chan", None)),
        check_vma=False,
    )
```

```python
import math

import jax
import jax.numpy as jnp
from jax import lax
from jax.experimental import pallas as pl
from jax.experimental.pallas import tpu as pltpu
from jax.sharding import PartitionSpec as P

MESH = pl.DeviceIdType.MESH
F32, BF16 = jnp.float32, jnp.bfloat16
NX, NYL, NZ, NYH = 4, 2, 8, 2
Y, Z = 16, 128
CELLS = Y * Z
ROWS = 16
ODD = 128
SPAN = 240.0


def tap_of(par, step):
    if par == 0:
        return 1 if step == 0 else None
    return 2 if step == 0 else 0


def taps_of_shift(shift):
    found = []
    for par in range(8):
        bits = (par // 4, par // 2 % 2, par % 2)
        taps = [tap_of(b, s) for b, s in zip(bits, shift)]
        if None not in taps:
            found.append((par, 9 * taps[0] + 3 * taps[1] + taps[2]))
    return found


PARTS = (
    ((0, 0, (0,)), (0, 1, (0,)), (1, 1, (0,))),
    ((1, 0, (0, 1)), (0, 0, (1,)), (0, 1, (1,)), (1, 1, (1,))),
)


def part_taps(part):
    return [
        tap for sy, sz, planes in PARTS[part] for sx in planes for _, tap in taps_of_shift((sx, sy, sz))
    ]


SHIFTS = [(sx, sy, sz) for sx in range(2) for sy in range(2) for sz in range(2)]


def encode(values):
    largest = jnp.max(jnp.abs(values), axis=-2, keepdims=True)
    scale = jnp.maximum((largest * 1.01).astype(BF16).astype(F32), 1e-30)
    level = values * (SPAN / scale)
    power = jnp.exp2(jnp.abs(level) - SPAN / 2)
    power = jnp.where(values < 0, -power, power)
    row = lax.broadcasted_iota(jnp.int32, values.shape, values.ndim - 2)
    return jnp.where(row >= ROWS - 2, scale, power).astype(BF16)


def decode(codes):
    codes = codes.astype(F32)
    scale = codes[..., ROWS - 2 : ROWS - 1, :] * (1.0 / SPAN)
    level = (jnp.log2(jnp.abs(codes)) + SPAN / 2) * scale
    return jnp.where(codes < 0, -level, level)


def kernel(
    norm, act_hbm, grad_hbm, weight_hbm, out_act, ag,
    act_ref, grad_ref, weight_ref, rows32, acts, before_maps, relay, grads, dense,
    terms, from_mate, rs_own, rs_out, rs_in,
    local, send_own, recv_own, send_rim, recv_rim, hop_send, hop_recv,
    rs_send, rs_recv, ag_send, ag_recv, fw_send, fw_recv, greeted,
):
    g, chan = lax.axis_index("grid"), lax.axis_index("chan")
    w, core = g >> 1, g & 1
    x, yl = chan >> 1, chan & 1
    last = 2 * NZ * NYH - 1

    def chan_of(dx, dy):
        return ((x + dx) & (NX - 1)) * NYL + (yl ^ dy)

    def at_chan(dx, dy):
        return (g, chan_of(dx, dy))

    mate = (g + 1 - 2 * core, chan)
    before = (jnp.maximum(g - 1, 0), chan)
    following = (jnp.minimum(g + 1, last), chan)

    def peer_w(d):
        return ((w & NZ) ^ (d & NZ)) + ((w + d) & (NZ - 1))

    def slot_of(d):
        return (d & NZ) + ((NZ - d) & (NZ - 1))

    def peer(d):
        return (peer_w(d) * 2 + core, chan)

    has_rim = jnp.logical_and(core == 1, g < last)
    gives_rim = jnp.logical_and(core == 0, g > 0)

    loads = [
        pltpu.make_async_copy(grad_hbm, grad_ref, local.at[0]),
        pltpu.make_async_copy(act_hbm, act_ref, local.at[1]),
        pltpu.make_async_copy(weight_hbm, weight_ref, local.at[2]),
    ]
    for c in loads:
        c.start()

    barrier = pltpu.get_barrier_semaphore()
    near = [at_chan(1, 0), at_chan(3, 0), at_chan(0, 1), at_chan(1, 1), at_chan(3, 1), mate]
    far_first = [d for high in (NZ, 0) for k in (4, 3, 5, 2, 6, 1, 7, 0) for d in (k + high,) if d]
    next_z, before_z, other_y = peer(1), peer(NZ - 1), peer(NZ)
    near += [next_z, before_z, other_y]
    for device in near:
        pl.semaphore_signal(barrier, inc=1, device_id=device, device_id_type=MESH)

    @pl.when(gives_rim)
    def _():
        pl.semaphore_signal(barrier, inc=1, device_id=before, device_id_type=MESH)

    @pl.when(has_rim)
    def _():
        pl.semaphore_signal(barrier, inc=1, device_id=following, device_id_type=MESH)

    @pl.when(g == 0)
    def _():
        pl.semaphore_signal(barrier, inc=1, device_id=(2 * NZ - 1, chan), device_id_type=MESH)

    @pl.when(g == 2 * NZ - 1)
    def _():
        pl.semaphore_signal(barrier, inc=1, device_id=(0, chan), device_id_type=MESH)

    def piece(plane, dx, dy, h):
        start = pl.multiple_of(chan_of(dx, dy) * 32 + 16 * h, 16)
        return grads.at[plane, 0, pl.ds(start, 16), pl.ds(0, CELLS)]

    loads[0].wait()
    rows32[0 : 32 * Y] = grad_ref[:, 0].astype(F32).reshape(32 * Y, Z)
    start_own = pl.multiple_of(chan * 32, 32)

    def along(j, size=Z):
        return pl.ds(pl.multiple_of(j * size, size), size)

    @pl.loop(0, Y)
    def _(j):
        grads[0, 0, pl.ds(start_own, 32), along(j)] = rows32[pl.ds(j, 32, stride=Y)].astype(BF16)

    rim_partners = jnp.logical_or(gives_rim, has_rim).astype(jnp.int32)
    rim_partners += jnp.logical_or(g == 0, g == 2 * NZ - 1).astype(jnp.int32)
    pl.semaphore_wait(barrier, len(near) + rim_partners)

    def copy(src, dst, send, recv, device):
        return pltpu.make_async_remote_copy(
            src_ref=src, dst_ref=dst, send_sem=send, recv_sem=recv,
            device_id=device, device_id_type=MESH,
        )

    def gather_copies(plane, send, recv):
        count = [0]

        def one(dx, dy, h, slot, device):
            n = count[0]
            count[0] += 1
            ref = piece(plane, dx, dy, h)
            return copy(ref, ref, send.at[n], recv.at[slot, h], device)

        own = []
        for h in range(2):
            own.append(one(0, 0, h, 1, at_chan(0, 1)))
            own.append(one(0, 0, h, 6, at_chan(1, 0)))
            own.append(one(0, 0, h, 2, at_chan(3, 0)))
        passed = []
        for h in range(2):
            passed.append(
                ((0, 1, h), [one(0, 1, h, 7, at_chan(1, 0)), one(0, 1, h, 3, at_chan(3, 0))])
            )
            dx = 3 - 2 * h
            passed.append(
                (
                    (dx, 0, h),
                    [one(dx, 0, h, 4, at_chan(4 - dx, 0)), one(dx, 0, h, 5, at_chan(4 - dx, 1))],
                )
            )
        return own, passed

    def wait_piece(plane, recv, slot, h):
        ref = piece(plane, 0, 0, h)
        pltpu.make_async_copy(ref, ref, recv.at[slot, h]).wait()

    own, passed = gather_copies(0, send_own, recv_own)
    rim_own, rim_passed = gather_copies(1, send_rim, recv_rim)
    rim_first = [
        copy(
            piece(0, 0, 0, h), piece(1, 0, 0, h), hop_send.at[h], recv_rim.at[0, h], before
        )
        for h in range(2)
    ]
    half_odd = ODD // 2
    crosses, relays = g == 2 * NZ - 1, g == 0
    relay_at = (0, chan)
    upper = acts.at[pl.ds(ODD + half_odd, half_odd)]
    arrives = before_maps.at[pl.ds(half_odd, half_odd)]
    odd_lower = copy(
        acts.at[pl.ds(ODD, half_odd)], before_maps.at[pl.ds(0, half_odd)],
        hop_send.at[2], hop_recv.at[0], following,
    )
    odd_upper = copy(upper, arrives, hop_send.at[4], hop_recv.at[2], following)
    odd_to_relay = copy(upper, relay, hop_send.at[4], hop_recv.at[3], relay_at)
    odd_relayed = copy(relay, arrives, hop_send.at[5], hop_recv.at[2], (2 * NZ, chan))
    plane_cells = pl.ds(0, CELLS)
    whole_plane = copy(
        grads.at[0, 0, :, plane_cells], grads.at[1, 0, :, plane_cells],
        hop_send.at[3], hop_recv.at[1], mate,
    )

    def greet(turn, *devices):
        for device in devices:
            pl.semaphore_signal(greeted.at[turn], inc=1, device_id=device, device_id_type=MESH)

    for c in own:
        c.start()
    greet(0, next_z, before_z)

    loads[1].wait()

    @pl.loop(0, 8)
    def _(par):
        rows32[along(par, 32 * Y)] = act_ref[:, 0, par].astype(F32).reshape(32 * Y, Z)

    for base in (ODD, 0):

        @pl.loop(0, Y)
        def _(j):
            acts[base : base + ODD, along(j)] = rows32[
                pl.ds(base * Y + j, ODD, stride=Y)
            ].astype(BF16)

        if base:

            @pl.when(g < last)
            def _():
                odd_lower.start()

            @pl.when(jnp.logical_and(g < last, jnp.logical_not(crosses)))
            def _():
                odd_upper.start()

            @pl.when(crosses)
            def _():
                odd_to_relay.start()

    @pl.when(gives_rim)
    def _():
        for c in rim_first:
            c.start()

    for plane in range(2):
        for sz in range(2):
            grads[plane, sz, :, CELLS:] = jnp.zeros((256, Z), BF16)

    @pl.when(g == last)
    def _():
        grads[1, 0, :, 0:CELLS] = jnp.zeros((256, CELLS), BF16)

    @pl.when(g == 0)
    def _():
        before_maps[...] = jnp.zeros_like(before_maps)

    terms[...] = jnp.zeros_like(terms)

    def pass_on(plane, recv, steps):
        for (dx, dy, h), copies in steps:
            wait_piece(plane, recv, dx * 2 + dy, h)
            for c in copies:
                c.start()

    pl.semaphore_wait(greeted.at[0], 2)
    greet(1, peer(2), peer(NZ - 2))
    pass_on(0, recv_own, passed)
    pl.semaphore_wait(greeted.at[1], 2)
    greet(2, other_y)

    @pl.when(relays)
    def _():
        odd_to_relay.wait_recv()
        odd_relayed.start()


    loads[2].wait()
    dense[...] = jnp.zeros_like(dense)
    for n, shift in enumerate(SHIFTS):
        for par, tap in taps_of_shift(shift):
            dense[par * 32 : (par + 1) * 32, n * 256 : (n + 1) * 256] = weight_ref[tap]

    lane = lax.broadcasted_iota(jnp.int32, (128, Z), 1)

    def shift_z(plane, half):
        start = pl.multiple_of(half * 128, 128)

        @pl.loop(0, Y)
        def _(j):
            block = grads[plane, 0, pl.ds(start, 128), along(j)].astype(F32)
            moved = pltpu.roll(block, Z - 1, 1)
            grads[plane, 1, pl.ds(start, 128), along(j)] = jnp.where(
                lane == Z - 1, 0.0, moved
            ).astype(BF16)

    def filter_terms(part):
        row = 0
        for sy, sz, planes in PARTS[part]:
            maps = []
            for sx in planes:
                for par, _ in taps_of_shift((sx, sy, sz)):
                    source, base = (before_maps, 4) if sx else (acts, 0)
                    maps.append(source[(par - base) * 32 : (par - base + 1) * 32])
            window = grads[0, sz, :, sy * Z : sy * Z + CELLS]
            product = lax.dot_general(
                jnp.concatenate(maps, 0), window, (((1,), (1,)), ((), ())),
                preferred_element_type=F32,
            )
            for n in range(len(maps)):
                for half in range(2):
                    terms[part, half, pl.ds(row, 32, stride=ROWS), :] = product[
                        n * 32 : (n + 1) * 32, half * 128 : (half + 1) * 128
                    ]
                row += 1

    mine = 16 * ROWS
    theirs = pl.multiple_of((1 - core) * mine, mine)
    ours = pl.multiple_of(core * mine, mine)
    to_mate = [
        copy(
            terms.at[part, :, pl.ds(theirs, mine)], from_mate.at[part],
            fw_send.at[part], fw_recv.at[part], mate,
        )
        for part in range(2)
    ]
    halves = [x // 2, 1 - x // 2]
    near_x = 1 + 2 * lax.rem(x, 2)
    far_x = 4 - near_x

    wait_piece(0, recv_own, 6, 1)
    wait_piece(0, recv_own, 2, 0)
    for h in range(2):
        wait_piece(0, recv_own, near_x * 2 + 1, h)
    shift_z(0, halves[0])
    for slot in (4, 5):
        for h in range(2):
            wait_piece(0, recv_own, slot, h)
    for h in range(2):
        wait_piece(0, recv_own, far_x * 2 + 1, h)
    shift_z(0, halves[1])
    filter_terms(0)
    to_mate[0].start()

    @pl.when(has_rim)
    def _():
        for h in range(2):
            wait_piece(1, recv_rim, 0, h)
        for c in rim_own:
            c.start()

    @pl.when(core == 1)
    def _():
        whole_plane.start()

    def scatter(part):
        to_mate[part].wait_recv()
        for half in range(2):
            total = terms[part, half, pl.ds(ours, mine), :] + from_mate[part, half]
            total = total.reshape(16, ROWS, 128)
            rs_own[part, :, half] = total
            rs_out[part, :, half] = encode(total)

        for d in far_first:
            copy(
                rs_out.at[part, peer_w(d)], rs_in.at[part, slot_of(d)],
                rs_send.at[part], rs_recv.at[part], peer(d),
            ).start()

    def wait_many(ref, sem):
        pltpu.make_async_copy(ref, ref, sem).wait()

    pl.semaphore_wait(greeted.at[2], 1)
    scatter(0)

    @pl.when(g > 0)
    def _():
        odd_lower.wait_recv()
        odd_upper.wait_recv()

    filter_terms(1)
    to_mate[1].start()
    scatter(1)

    @pl.when(has_rim)
    def _():
        pass_on(1, recv_rim, rim_passed)

    def share(part):
        wait_many(rs_in.at[part, pl.ds(1, 15)], rs_recv.at[part])
        total = rs_own[part, w] + jnp.sum(decode(rs_in[part, 1:16]), axis=0)
        ag[part, core, w] = encode(total * norm)

        for d in far_first:
            block = ag.at[part, core, w]
            copy(block, block, ag_send.at[part], ag_recv.at[part], peer(d)).start()

    share(0)
    share(1)

    @pl.when(has_rim)
    def _():
        for slot, h in ((6, 1), (2, 0)):
            wait_piece(1, recv_rim, slot, h)
        for slot in (3, 4, 5, 7):
            for h in range(2):
                wait_piece(1, recv_rim, slot, h)

    @pl.when(core == 0)
    def _():
        whole_plane.wait_recv()

    for half in range(2):
        shift_z(1, half)

    @pl.loop(0, CELLS // 256)
    def _(tile):
        columns = []
        for sx, sy, sz in SHIFTS:
            cells = pl.ds(pl.multiple_of(tile * 256 + sy * Z, Z), 256)
            columns.append(grads[sx, sz, :, cells])
        window = jnp.concatenate(columns, 0)
        sums = jnp.dot(dense[...], window, preferred_element_type=F32)
        for j in range(2):
            rows32[pl.ds(tile * 2 + j, 256, stride=Y)] = sums[:, j * Z : (j + 1) * Z]

    @pl.loop(0, 8)
    def _(par):
        out_act[:, 0, par] = rows32[along(par, 32 * Y)].reshape(32, Y, Z).astype(BF16)

    ag_mate = []
    for part in range(2):
        wait_many(ag.at[part, core, pl.ds(0, 15)], ag_recv.at[part])
        c = copy(
            ag.at[part, core], ag.at[part, core],
            fw_send.at[2 + part], fw_recv.at[2 + part], mate,
        )
        c.start()
        ag_mate.append(c)
    for c in ag_mate:
        c.wait_recv()

    sent = own + [c for _, copies in passed for c in copies]
    for c in sent + to_mate + ag_mate:
        c.wait_send()
    for part in range(2):
        wait_many(rs_out.at[part, pl.ds(1, 15)], rs_send.at[part])
        wait_many(ag.at[part, core, pl.ds(1, 15)], ag_send.at[part])

    @pl.when(has_rim)
    def _():
        for c in rim_own + [c for _, copies in rim_passed for c in copies]:
            c.wait_send()

    @pl.when(gives_rim)
    def _():
        for c in rim_first:
            c.wait_send()

    @pl.when(g < last)
    def _():
        odd_lower.wait_send()
        odd_upper.wait_send()

    @pl.when(relays)
    def _():
        odd_relayed.wait_send()

    @pl.when(core == 1)
    def _():
        whole_plane.wait_send()


def finish(codes, act_ref, out_act, out_w, terms, result, sems):
    moved = pltpu.make_async_copy(act_ref, out_act, sems.at[0])
    moved.start()
    span, written = 16 * 2 * ROWS, []
    for core in range(2):
        for part in range(2):
            terms[part] = decode(codes[part, core]).reshape(span, 128)
            for row, tap in enumerate(part_taps(part)):
                for half in range(2):
                    result[tap, core * 16 : (core + 1) * 16, half * 128 : (half + 1) * 128] = (
                        terms[part, pl.ds(half * ROWS + row, 16, stride=2 * ROWS)]
                    )
        rows = pl.ds(core * 16, 16)
        c = pltpu.make_async_copy(result.at[:, rows], out_w.at[:, rows], sems.at[1 + core])
        c.start()
        written.append(c)
    moved.wait()
    for c in written:
        c.wait()


def on_device(activations, grad_out, weight):
    _, planes, _, out_y, out_z = activations.shape
    norm = 1.0 / math.sqrt(planes * out_y * out_z * lax.axis_size("grid"))
    vmem = pl.BlockSpec(memory_space=pltpu.VMEM)
    anywhere = pl.BlockSpec(memory_space=pl.ANY)
    dma = pltpu.SemaphoreType.DMA
    maps = jax.ShapeDtypeStruct(activations.shape, BF16)
    code_shape = (2, 2, 16, 2, ROWS, 128)
    grad_act, codes = pl.pallas_call(
        lambda *refs: kernel(norm, *refs),
        out_shape=(maps, jax.ShapeDtypeStruct(code_shape, BF16)),
        in_specs=[pl.BlockSpec(memory_space=pltpu.HBM)] * 3,
        out_specs=(vmem, vmem),
        scratch_shapes=[
            pltpu.VMEM(activations.shape, BF16),
            pltpu.VMEM(grad_out.shape, BF16),
            pltpu.VMEM(weight.shape, BF16),
            pltpu.VMEM((256 * Y, Z), F32),
            pltpu.VMEM((256, CELLS), BF16),
            pltpu.VMEM((ODD, CELLS), BF16),
            pltpu.VMEM((ODD // 2, CELLS), BF16),
            pltpu.VMEM((2, 2, 256, CELLS + Z), BF16),
            pltpu.VMEM((256, 2048), BF16),
            pltpu.VMEM((2, 2, 32 * ROWS, 128), F32),
            pltpu.VMEM((2, 2, 16 * ROWS, 128), F32),
            pltpu.VMEM((2, 16, 2, ROWS, 128), F32),
            pltpu.VMEM((2, 16, 2, ROWS, 128), BF16),
            pltpu.VMEM((2, 16, 2, ROWS, 128), BF16),
            dma((3,)), dma((14,)), dma((8, 2)), dma((14,)), dma((8, 2)), dma((6,)), dma((4,)),
            dma((2,)), dma((2,)), dma((2,)), dma((2,)), dma((4,)), dma((4,)),
            pltpu.SemaphoreType.REGULAR((3,)),
        ],
        compiler_params=pltpu.CompilerParams(
            collective_id=0, has_side_effects=True, vmem_limit_bytes=48 << 20
        ),
    )(*(pltpu.with_memory_space_constraint(v, pltpu.HBM) for v in (activations, grad_out, weight)))
    return pl.pallas_call(
        finish,
        out_shape=(maps, jax.ShapeDtypeStruct(weight.shape, F32)),
        in_specs=[vmem, vmem],
        out_specs=(anywhere, anywhere),
        scratch_shapes=[
            pltpu.VMEM((2, 16 * 2 * ROWS, 128), F32),
            pltpu.VMEM(weight.shape, F32),
            dma((3,)),
        ],
        compiler_params=pltpu.CompilerParams(vmem_limit_bytes=16 << 20),
    )(codes, grad_act)


def solution(mesh):
    placed = (
        P("chan", "grid", None, None, None),
        P("chan", "grid", None, None),
        P(None, "chan", None),
    )
    return jax.shard_map(
        on_device,
        mesh=mesh,
        in_specs=placed,
        out_specs=(P("chan", "grid", None, None, None), P(None, "chan", None)),
        check_vma=False,
    )
```
